128 devices in a mesh: grp: 8 (over y, core), blk: 16 (over z, x).
Axes of the slice: x: 4, y: 4, z: 4, core: 2. Of those that a mesh axis runs over, the one named last changes fastest.
Arguments:
- embeddings: bfloat16 [49152, 1024], P(('grp', 'blk')), may hold values from -6 to 6
- routes: int32 [49152, 1], P(('grp', 'blk')), may hold values from 0 to 127; in each aligned block of 384 rows (0 to 383, 384 to 767, ...) at most 6 rows name the same one
- ranks: int32 [49152], P(('grp', 'blk')), may hold values from 0 to 49151, each once
Outputs:
- similarity: float32 [49152], P(('grp', 'blk'))
The draws below stay inside these ranges and needn't reach their ends.
Inputs may be any that keep to these rules, and one draw needn't show every extreme that they name: `routes`: in the rows of one home device, at most 6 documents name the same target, and some home device reaches this bound. `ranks`: A permutation of all document numbers.
All inputs are finite; a program needn't handle non-finite values.
Results may differ from the reference program's by a relative error of at most 0.0013.
Values may be sent and summed in bfloat16 or wider, within the bound.
A program may use at most 128 MiB of HBM per device.

```python
import math
import jax
import jax.numpy as jnp
import numpy as np
from jax import lax

D = 1024
DOC_DEV = 384
DOCS = 49152
SLOT = 6
N_BLK = 16
DEVICES = 128


def steps_of(key, shape, shards, least, top_value):
    level = 1.0
    for dim, parts in shards:
        heights = jax.random.uniform(jax.random.fold_in(jax.random.fold_in(key, 6), dim), (parts,), jnp.float32, least / len(shards), top_value / len(shards))
        level = level * jnp.repeat(jnp.exp(heights), shape[dim] // parts).reshape((-1,) + (1,) * (len(shape) - 1 - dim))
    return level


def routed_block(rng, own, number, rows, count, top, most, skew):
    sequence = jax.random.permutation(rng, count)
    heavy_load, ordinary = portions_of(count, rows * top, most, skew, True), portions_of(count, rows * top, most, skew, False)
    places = jnp.arange(count)

    def named(tallies, turn):
        used = int((tallies > 0).sum())
        fixed = max(1, used // 4)
        passed = fixed + (places - fixed + turn * (used - fixed)) % max(1, count - fixed)
        return jnp.zeros((count,), jnp.int32).at[sequence[jnp.where(places < fixed, places, passed)]].set(jnp.asarray(tallies, jnp.int32))

    tallies = jnp.where(number % 4 == 0, named(heavy_load, number // 4), named(ordinary, number - number // 4 - 1))
    mixed = jax.random.permutation(jax.random.fold_in(own, 3), count)
    source_of, taker = mixed[0:count // 2 * 2:2], mixed[1:count // 2 * 2:2]
    margin = jnp.minimum(tallies[source_of] - 1, most - tallies[taker]) // 2
    margin = jnp.where((source_of == sequence[0]) | (taker == sequence[0]) | (tallies[taker] == 0), 0, jnp.maximum(margin, 0))
    passed = jax.random.randint(jax.random.fold_in(own, 4), (count // 2,), 0, 1 << 20) % (margin + 1)
    tallies = tallies.at[source_of].add(-passed).at[taker].add(passed)
    items = jnp.searchsorted(jnp.cumsum(tallies), jnp.arange(rows * top), side="right").astype(jnp.int32)
    grid = items.reshape(top, rows).T
    grid = grid[jax.random.permutation(jax.random.fold_in(own, 1), rows)]
    turn = jax.random.randint(jax.random.fold_in(own, 2), (rows, 1), 0, top)
    return jnp.take_along_axis(grid, (jnp.arange(top)[None, :] + turn) % top, axis=1)


def portions_of(amount, total, most, slope, full):
    weights = [(1 << 20) // math.isqrt(rank ** slope) + 1 for rank in range(1, amount + 1)]
    largest = most if full else min(most, max(-(-total // amount), total * weights[0] // sum(weights)))
    least = 1 if total - largest >= amount - 1 else 0
    counts, surplus = [largest] + [least] * (amount - 1), total - largest - least * (amount - 1)
    while surplus > 0:
        movable = [i for i in range(1, amount) if counts[i] < largest] or [i for i in range(1, amount) if counts[i] < most]
        whole, left = sum([weights[i] for i in movable]), surplus
        for i in movable:
            more = min(most - counts[i], max(1, left * weights[i] // whole), surplus)
            counts[i] = counts[i] + more
            surplus = surplus - more
    return np.array(counts)


def gaussian(stream_key, extent, spread, limit, cuts=(), kind=jnp.bfloat16):
    array = jax.random.normal(stream_key, extent, jnp.float32) * spread
    if len(cuts) > 0:
        array = steps_of(stream_key, extent, cuts, -0.22, 0.18) * array
    return jnp.clip(array, min=-limit, max=limit).astype(kind)


def setup_inputs(seed: int = 0) -> dict:
    key_list = jax.random.split(jax.random.key(seed), 4)
    embeddings = gaussian(key_list[0], (DOCS, D), 1.0, 6.0, ((0, 128),))
    routes_keys = jax.random.split(jax.random.fold_in(key_list[1], 1), DOCS // DOC_DEV)
    routes_turns = jax.random.permutation(jax.random.fold_in(key_list[1], 3), DOCS // DOC_DEV)
    routes = jax.vmap(lambda own, number: routed_block(jax.random.fold_in(key_list[1], 2), own, number, DOC_DEV, DEVICES, 1, SLOT, 2))(routes_keys, routes_turns).reshape((DOCS, 1))
    ranks = jax.random.permutation(key_list[2], DOCS).astype(jnp.int32)
    return dict(embeddings=embeddings, routes=routes, ranks=ranks)


def reference(embeddings, routes, ranks):
    values = embeddings.astype(jnp.float32)
    unit = (values * lax.rsqrt(lax.optimization_barrier(jnp.sum(values * values, axis=1, keepdims=True)) + 1e-06)).astype(jnp.bfloat16)
    cluster = (routes[:, 0] // N_BLK).astype(jnp.int32)
    order = jnp.argsort(cluster * DOCS + ranks).astype(jnp.int32)
    sorted_unit = unit[order].astype(jnp.float32)
    sorted_cluster = cluster[order]
    sorted_rank = ranks[order]
    row_block = min(512, DOCS)
    window = min(DOCS, 2 * DOC_DEV * N_BLK + row_block)

    def block(index):
        first = (index * row_block).astype(jnp.int32)
        start = jnp.clip(first + row_block - window, 0, DOCS - window).astype(jnp.int32)
        rows = lax.dynamic_slice_in_dim(sorted_unit, first, row_block, 0)
        row_cluster = lax.dynamic_slice_in_dim(sorted_cluster, first, row_block, 0)
        row_rank = lax.dynamic_slice_in_dim(sorted_rank, first, row_block, 0)
        cols = lax.dynamic_slice_in_dim(sorted_unit, start, window, 0)
        col_cluster = lax.dynamic_slice_in_dim(sorted_cluster, start, window, 0)
        col_rank = lax.dynamic_slice_in_dim(sorted_rank, start, window, 0)
        score = jnp.dot(rows, cols.T, preferred_element_type=jnp.float32)
        keep = (col_cluster[None, :] == row_cluster[:, None]) & (col_rank[None, :] < row_rank[:, None])
        return lax.optimization_barrier(jnp.max(jnp.where(keep, score, jnp.float32(-1.0)), axis=1))
    best = lax.map(block, jnp.arange(DOCS // row_block, dtype=jnp.int32)).reshape(DOCS)
    return jnp.zeros((DOCS,), jnp.float32).at[order].set(best)
```

```python
import jax
import jax.numpy as jnp
from jax import lax
from jax.experimental import pallas as pl
from jax.experimental.pallas import tpu as pltpu
from jax.sharding import PartitionSpec as P

MESH = pl.DeviceIdType.MESH
D = 1024
DOC = 384
NSLOT = 8
LANES = 128
LATE = float(1 << 20)
DY = (0, 0, 1, 3, 1, 3, 2, 2)
ZZ = (0, 1, 0, 0, 1, 1, 0, 1)
OWN, LEFT, RIGHT, DIAG, BLOCKS = 0, 2, 4, 6, 7


def xor(a, b):
    return a + b - 2 * a * b


def kernel(cap, emb_ref, route_ref, rank_ref, out_ref, unit, pack, send, msg, seen, blk, rks, rcol, rrow, racc, cacc,
           part, rpart, fin, home, s1, r1, sk, rk, sx, rx, sq, rq, sp, rp, sf, rf):
    n = NSLOT * cap
    g, b = lax.axis_index("grp"), lax.axis_index("blk")
    y, k, z, x = g // 2, g % 2, b // 4, b % 4
    o = 1 - k
    zin, zout = z + 1 - 2 * (z % 2), 3 - z
    xp, xm = (x + 1) % 4, (x + 3) % 4
    lsel, rsel = LEFT + xor(k, x // 2), RIGHT + xor(k, z % 2)

    def at(yy, kk, zz, xx):
        return (yy * 2 + kk, zz * 4 + xx)

    def target(i):
        return at((y + DY[i]) % 4, k, zout if ZZ[i] else z, x)

    def source(i):
        return at((y + 4 - DY[i]) % 4, k, zout if ZZ[i] else z, x)

    left, right, sibling, inner = at(y, k, z, xm), at(y, k, z, xp), at(y, o, z, x), at(y, k, zin, x)

    def remote(src, dst, ss, rs, to):
        return pltpu.make_async_remote_copy(src_ref=src, dst_ref=dst, send_sem=ss, recv_sem=rs, device_id=to, device_id_type=MESH)

    barrier = pltpu.get_barrier_semaphore()
    partners = [target(i) for i in range(1, NSLOT)] + [left, right, sibling, inner]
    partners += [at(y, o, z, xm), at(y, o, z, xp), at(y, k, zin, xm), at(y, k, zin, xp)]
    for to in partners:
        pl.semaphore_signal(barrier, inc=1, device_id=to, device_id_type=MESH)

    values = emb_ref[...].astype(jnp.float32)
    unit[...] = (values * lax.rsqrt(jnp.sum(values * values, axis=1, keepdims=True) + 1e-06)).astype(jnp.bfloat16)
    cluster = route_ref[...] // 16
    index = jnp.zeros((1, DOC), jnp.int32)
    for i in range(1, NSLOT):
        zz = zout if ZZ[i] else z
        index = jnp.where(cluster == ((y + DY[i]) % 4) * 2 + zz // 2, i, index)
    chosen = index == lax.broadcasted_iota(jnp.int32, (NSLOT, DOC), 0)
    onehot = jnp.where(chosen, 1.0, 0.0)
    before = lax.broadcasted_iota(jnp.int32, (DOC, DOC), 0) < lax.broadcasted_iota(jnp.int32, (DOC, DOC), 1)
    counts = jnp.dot(onehot.astype(jnp.bfloat16), jnp.where(before, 1.0, 0.0).astype(jnp.bfloat16),
                     preferred_element_type=jnp.float32)
    position = jnp.sum(counts * onehot, axis=0, keepdims=True).astype(jnp.int32)
    place = index * LANES + position
    for i in range(NSLOT):
        hit = place == lax.broadcasted_iota(jnp.int32, (LANES, DOC), 0) + i * LANES
        pack[i * LANES:(i + 1) * LANES, :] = jnp.where(hit, 1.0, 0.0).astype(jnp.bfloat16)

    rank = rank_ref[...]
    line = lax.broadcasted_iota(jnp.int32, (8, DOC), 0)
    digits = jnp.where(line == 0, rank // 256, jnp.where(line == 1, rank % 256, 1)).astype(jnp.float32).astype(jnp.bfloat16)
    placed = lax.dot_general(digits, pack[...], (((1,), (1,)), ((), ())), preferred_element_type=jnp.float32)
    slot_rank = placed[0:1] * 256.0 + placed[1:2] + (1.0 - placed[2:3]) * LATE
    sub, lane = lax.broadcasted_iota(jnp.int32, (8, LANES), 0), lax.broadcasted_iota(jnp.int32, (8, LANES), 1)
    for i in range(NSLOT):
        row = jnp.broadcast_to(slot_rank[:, i * LANES:(i + 1) * LANES], (8, LANES))
        msg[i] = jnp.where((sub == i) & (lane < cap), row, LATE)
    seen[0] = msg[0]

    def rows(i):
        return pl.ds(i * cap, cap)

    first = [None] + [remote(send.at[i], blk.at[OWN + k, rows(i)], s1.at[i], r1.at[i], target(i)) for i in range(1, NSLOT)]
    rank1 = [None] + [remote(msg.at[i], seen.at[i], sk.at[i], rk.at[i], target(i)) for i in range(1, NSLOT)]

    def route(kind, src, dst, to):
        return [remote(blk.at[src, rows(i)], blk.at[dst, rows(i)], sx.at[kind, i], rx.at[kind, i], to) for i in range(NSLOT)], \
            remote(rks.at[src], rks.at[dst], sq.at[kind], rq.at[kind], to)

    to_left, rank_left = route(0, OWN + k, RIGHT + k, left)
    to_right, rank_right = route(1, OWN + k, LEFT + k, right)
    to_sib, rank_sib = route(2, OWN + k, OWN + k, sibling)
    to_inner, rank_inner = route(3, RIGHT + k, DIAG, inner)
    sib_right, rank_sib_right = route(4, RIGHT + k, RIGHT + k, sibling)
    sib_left, rank_sib_left = route(5, LEFT + k, LEFT + k, sibling)

    racc[...] = jnp.full(racc.shape, -1.0, jnp.float32)
    cacc[...] = jnp.full(cacc.shape, -1.0, jnp.float32)
    pl.semaphore_wait(barrier, len(partners))

    for i in range(1, NSLOT):
        rank1[i].start()
    for i in range(NSLOT):
        batch = jnp.dot(pack[i * LANES:i * LANES + cap, :], unit[...], preferred_element_type=jnp.float32).astype(jnp.bfloat16)
        if i == 0:
            blk[OWN + k, 0:cap, :] = batch
            for copies in (to_left, to_right, to_sib):
                copies[0].start()
        else:
            send[i] = batch
            first[i].start()

    def spread(block):
        tile = rks[block]
        for j in range(n // LANES):
            line = jnp.full((8, LANES), LATE, jnp.float32)
            for i in range(NSLOT):
                start = i * cap - j * LANES
                if -cap < start < LANES:
                    piece = jnp.broadcast_to(tile[i:i + 1], (8, LANES))
                    if start % LANES:
                        piece = pltpu.roll(piece, start % LANES, 1)
                    line = jnp.where((lane >= start) & (lane < start + cap), piece, line)
            rcol[block, :, j * LANES:(j + 1) * LANES] = line
            rrow[block, j * LANES:(j + 1) * LANES, :] = jnp.broadcast_to(line[0:1], (LANES, LANES)).T

    for i in range(1, NSLOT):
        rank1[i].wait_recv()
    tile = seen[0]
    for i in range(1, NSLOT):
        tile = jnp.minimum(tile, seen[i])
    rks[OWN + k] = tile
    for copy in (rank_left, rank_right, rank_sib):
        copy.start()
    spread(OWN + k)

    def relay(i):
        to_left[i].wait_recv()
        to_inner[i].start()
        sib_right[i].start()
        to_right[i].wait_recv()
        sib_left[i].start()

    for i in range(1, NSLOT):
        first[i].wait_recv()
        for copies in (to_left, to_right, to_sib):
            copies[i].start()
        if i == 2:
            rank_left.wait_recv()
            rank_inner.start()
            rank_sib_right.start()
            rank_right.wait_recv()
            rank_sib_left.start()
            spread(RIGHT + k)
        if i >= 2:
            relay(i - 2)

    def block_pair(row_block, col_block, start, width, row_start=0, row_count=n, both=True):
        span = pl.ds(row_start, row_count)
        score = lax.dot_general(blk[row_block, span, :], blk[col_block, start:start + width, :], (((1,), (1,)), ((), ())),
                                preferred_element_type=jnp.float32)
        row_rank, best = rrow[row_block, span, :], racc[row_block, span, :]
        for c in range(0, width, LANES):
            col = slice(start + c, start + c + LANES)
            part_score = score[:, c:c + LANES]
            keep = rcol[col_block, 0:1, col] < row_rank
            best = jnp.maximum(best, jnp.where(keep, part_score, -1.0))
            if both:
                rest = jnp.where(keep, -1.0, part_score).reshape(row_count // 8, 8, LANES)
                cacc[col_block, :, col] = jnp.maximum(cacc[col_block, :, col], jnp.max(rest, axis=0))
        racc[row_block, span, :] = best

    chunks = [(c, min(256, n - c)) for c in range(0, n, 256)]

    def covered(c, w):
        return -(-(c + w) // cap)

    for c, w in chunks:
        block_pair(OWN + k, OWN + k, c, w, both=False)

    sib_block = [remote(blk.at[OWN + o, rows(i)], blk.at[OWN + o, rows(i)], sx.at[2, i], rx.at[2, i], sibling) for i in range(NSLOT)]
    rsib = {kind: [remote(blk.at[dst, rows(i)], blk.at[dst, rows(i)], sx.at[kind, i], rx.at[kind, i], sibling) for i in range(NSLOT)]
            for kind, dst in ((4, RIGHT + o), (5, LEFT + o))}
    rsib_rank = {kind: remote(rks.at[dst], rks.at[dst], sq.at[kind], rq.at[kind], sibling)
                 for kind, dst in ((2, OWN + o), (4, RIGHT + o), (5, LEFT + o))}
    rsib_rank[2].wait_recv()
    spread(OWN + o)
    for i in range(NSLOT):
        sib_block[i].wait_recv()
    half = n // 2
    for c, w in chunks:
        block_pair(OWN, OWN + 1, c, w, row_start=pl.multiple_of(k * half, half), row_count=half)

    rank_inner.wait_recv()
    spread(DIAG)
    rsib_rank[4].wait_recv()
    spread(RIGHT + o)
    spread(LEFT + k)
    rsib_rank[5].wait_recv()
    spread(LEFT + o)

    def own_rows(col_block, c, w):
        def step(j, carry):
            block_pair(OWN + j, col_block, c, w)
            return carry
        lax.fori_loop(0, 2, step, 0)

    relayed, arrived = 6, 0
    for c, w in chunks:
        while relayed < covered(c, w):
            relay(relayed)
            relayed += 1
        own_rows(RIGHT + k, c, w)
        if c + w < n:
            while arrived < covered(c, w):
                to_inner[arrived].wait_recv()
                arrived += 1
            own_rows(DIAG, c, w)
    for i in range(NSLOT):
        rsib[4][i].wait_recv()
        rsib[5][i].wait_recv()

    for c, w in chunks:
        block_pair(lsel, RIGHT + k, c, w)

    def side_rows(c, w):
        def step(j, carry):
            block_pair(jnp.where(j == 0, lsel, rsel), DIAG, c, w)
            return carry
        lax.fori_loop(0, 2, step, 0)

    for c, w in chunks:
        if c + w == n:
            while arrived < NSLOT:
                to_inner[arrived].wait_recv()
                arrived += 1
            own_rows(DIAG, c, w)
        side_rows(c, w)

    def folded(block):
        lines = []
        for j in range(n // LANES):
            span = slice(j * LANES, (j + 1) * LANES)
            by_row = jnp.max(racc[block, span, :].T, axis=0, keepdims=True)
            lines.append(jnp.broadcast_to(jnp.maximum(by_row, jnp.max(cacc[block, :, span], axis=0, keepdims=True)), (8, LANES)))
        tile = jnp.full((8, LANES), -1.0, jnp.float32)
        for i in range(NSLOT):
            for j in range(n // LANES):
                start = j * LANES - i * cap
                if -LANES < start < cap:
                    piece = lines[j]
                    if start % LANES:
                        piece = pltpu.roll(piece, start % LANES, 1)
                    tile = jnp.where((sub == i) & (lane >= start) & (lane < min(cap, start + LANES)), piece, tile)
        return tile

    ends = ((OWN + o, sibling, sibling), (lsel, at(y, xor(k, x // 2), z, xm), left), (RIGHT + k, right, left),
            (rsel, at(y, xor(k, z % 2), z, xp), left), (DIAG, at(y, k, zin, xp), left))
    copies = []
    for j, (block, to, _) in enumerate(ends):
        part[j] = folded(block)
        copies.append(remote(part.at[j], rpart.at[j], sp.at[j], rp.at[j], to))
        copies[-1].start()
    best = folded(OWN + k)
    for j, copy in enumerate(copies):
        copy.wait_recv()
        best = jnp.maximum(best, rpart[j])
    fin[...] = best
    back = [None] + [remote(fin, home.at[i], sf.at[i], rf.at[i], source(i)) for i in range(1, NSLOT)]
    for i in range(1, NSLOT):
        back[i].start()
    home[0] = best

    for i in range(NSLOT):
        if i:
            first[i].wait_send()
            rank1[i].wait_send()
        for group in (to_left, to_right, to_sib, to_inner, sib_right, sib_left):
            group[i].wait_send()
    for copy in (rank_left, rank_right, rank_sib, rank_inner, rank_sib_right, rank_sib_left, *copies):
        copy.wait_send()

    lines = []
    for i in range(NSLOT):
        if i:
            back[i].wait_recv()
        value = home[i, i:i + 1, :]
        high = value.astype(jnp.bfloat16).astype(jnp.float32)
        middle = (value - high).astype(jnp.bfloat16).astype(jnp.float32)
        low = value - high - middle
        lines.append(jnp.where(sub == 0, high, jnp.where(sub == 1, middle, jnp.where(sub == 2, low, 0.0))).astype(jnp.bfloat16))
    picked = jnp.dot(jnp.concatenate(lines, axis=1), pack[...], preferred_element_type=jnp.float32)
    out_ref[...] = picked[0:1] + picked[1:2] + picked[2:3]
    for i in range(1, NSLOT):
        back[i].wait_send()


def nearest(cap, embeddings, routes, ranks):
    n = NSLOT * cap
    f32, bf16 = jnp.float32, jnp.bfloat16
    dma = pltpu.SemaphoreType.DMA
    vmem = pl.BlockSpec(memory_space=pltpu.VMEM)
    return pl.pallas_call(
        lambda *refs: kernel(cap, *refs),
        out_shape=jax.ShapeDtypeStruct((1, DOC), f32),
        in_specs=[vmem] * 3,
        out_specs=vmem,
        scratch_shapes=[
            pltpu.VMEM((DOC, D), bf16),
            pltpu.VMEM((NSLOT * LANES, DOC), bf16),
            pltpu.VMEM((NSLOT, cap, D), bf16),
            pltpu.VMEM((NSLOT, 8, LANES), f32),
            pltpu.VMEM((NSLOT, 8, LANES), f32),
            pltpu.VMEM((BLOCKS, n, D), bf16),
            pltpu.VMEM((BLOCKS, 8, LANES), f32),
            pltpu.VMEM((BLOCKS, 8, n), f32),
            pltpu.VMEM((BLOCKS, n, LANES), f32),
            pltpu.VMEM((BLOCKS, n, LANES), f32),
            pltpu.VMEM((BLOCKS, 8, n), f32),
            pltpu.VMEM((5, 8, LANES), f32),
            pltpu.VMEM((5, 8, LANES), f32),
            pltpu.VMEM((8, LANES), f32),
            pltpu.VMEM((NSLOT, 8, LANES), f32),
            dma((NSLOT,)), dma((NSLOT,)), dma((NSLOT,)), dma((NSLOT,)),
            dma((6, NSLOT)), dma((6, NSLOT)), dma((6,)), dma((6,)),
            dma((5,)), dma((5,)), dma((NSLOT,)), dma((NSLOT,)),
        ],
        compiler_params=pltpu.CompilerParams(collective_id=1, has_side_effects=True, vmem_limit_bytes=56 * 2**20),
        cost_estimate=pl.CostEstimate(flops=17 * n * n * D, bytes_accessed=2 * DOC * D, transcendentals=DOC),
    )(embeddings, routes.reshape(1, DOC), ranks.reshape(1, DOC))


def body(embeddings, routes, ranks):
    return nearest(96, embeddings, routes, ranks).reshape(DOC)


def solution(mesh):
    in_specs = (P(("grp", "blk"), None), P(("grp", "blk"), None), P(("grp", "blk")))
    return jax.shard_map(body, mesh=mesh, in_specs=in_specs, out_specs=P(("grp", "blk")), check_vma=False)
```

```python
import jax
import jax.numpy as jnp
from jax import lax
from jax.experimental import pallas as pl
from jax.experimental.pallas import tpu as pltpu
from jax.sharding import PartitionSpec as P

MESH = pl.DeviceIdType.MESH
D = 1024
DOC = 384
NSLOT = 8
LANES = 128
LATE = float(1 << 20)
DY = (0, 0, 1, 3, 1, 3, 2, 2)
ZZ = (0, 1, 0, 0, 1, 1, 0, 1)
OWN, LEFT, RIGHT, DIAG, BLOCKS = 0, 2, 4, 6, 7
GROUPS = ((0,), (1, 2, 3, 6), (7, 4, 5))
PIECES = 2
LAG = 4
RANKS = 10
UNITS = tuple((i, p) for group in GROUPS for p in range(PIECES) for i in group)
FLAG = LANES - 1


def xor(a, b):
    return a + b - 2 * a * b


def kernel(cap, emb_ref, route_ref, rank_ref, out_ref, unit, pack, send, msg, seen, blk, rks, rcol, rrow, racc, cacc,
           part, rpart, fin, home, s1, r1, sk, rk, sx, rx, sq, rq, sp, rp, sf, rf):
    n = NSLOT * cap
    g, b = lax.axis_index("grp"), lax.axis_index("blk")
    y, k, z, x = g // 2, g % 2, b // 4, b % 4
    o = 1 - k
    zin, zout = z + 1 - 2 * (z % 2), 3 - z
    xp, xm = (x + 1) % 4, (x + 3) % 4
    lsel, rsel = LEFT + xor(k, x // 2), RIGHT + xor(k, z % 2)

    def at(yy, kk, zz, xx):
        return (yy * 2 + kk, zz * 4 + xx)

    def target(i):
        return at((y + DY[i]) % 4, k, zout if ZZ[i] else z, x)

    def source(i):
        return at((y + 4 - DY[i]) % 4, k, zout if ZZ[i] else z, x)

    left, right, sibling, inner = at(y, k, z, xm), at(y, k, z, xp), at(y, o, z, x), at(y, k, zin, x)

    def remote(src, dst, ss, rs, to):
        return pltpu.make_async_remote_copy(src_ref=src, dst_ref=dst, send_sem=ss, recv_sem=rs, device_id=to, device_id_type=MESH)

    barrier = pltpu.get_barrier_semaphore()
    partners = [target(i) for i in range(1, NSLOT)] + [left, right, sibling, inner]
    partners += [at(y, o, z, xm), at(y, o, z, xp), at(y, k, zin, xm), at(y, k, zin, xp)]
    for to in partners:
        pl.semaphore_signal(barrier, inc=1, device_id=to, device_id_type=MESH)

    values = emb_ref[...].astype(jnp.float32)
    unit[...] = (values * lax.rsqrt(jnp.sum(values * values, axis=1, keepdims=True) + 1e-06)).astype(jnp.bfloat16)
    cluster = route_ref[...] // 16
    index = jnp.zeros((1, DOC), jnp.int32)
    for i in range(1, NSLOT):
        zz = zout if ZZ[i] else z
        index = jnp.where(cluster == ((y + DY[i]) % 4) * 2 + zz // 2, i, index)
    chosen = index == lax.broadcasted_iota(jnp.int32, (NSLOT, DOC), 0)
    onehot = jnp.where(chosen, 1.0, 0.0)
    before = lax.broadcasted_iota(jnp.int32, (DOC, DOC), 0) < lax.broadcasted_iota(jnp.int32, (DOC, DOC), 1)
    counts = jnp.dot(onehot.astype(jnp.bfloat16), jnp.where(before, 1.0, 0.0).astype(jnp.bfloat16),
                     preferred_element_type=jnp.float32)
    position = jnp.sum(counts * onehot, axis=0, keepdims=True).astype(jnp.int32)
    place = index * LANES + position
    most = jnp.max(position, axis=1, keepdims=True)
    for i in range(NSLOT):
        hit = place == lax.broadcasted_iota(jnp.int32, (LANES, DOC), 0) + i * LANES
        pack[i * LANES:(i + 1) * LANES, :] = jnp.where(hit, 1.0, 0.0).astype(jnp.bfloat16)

    rank = rank_ref[...].reshape(1, DOC)
    line = lax.broadcasted_iota(jnp.int32, (8, DOC), 0)
    digits = jnp.where(line == 0, rank // 256, jnp.where(line == 1, rank % 256, 1)).astype(jnp.float32).astype(jnp.bfloat16)
    placed = lax.dot_general(digits, pack[...], (((1,), (1,)), ((), ())), preferred_element_type=jnp.float32)
    slot_rank = placed[0:1] * 256.0 + placed[1:2] + (1.0 - placed[2:3]) * LATE
    sub, lane = lax.broadcasted_iota(jnp.int32, (8, LANES), 0), lax.broadcasted_iota(jnp.int32, (8, LANES), 1)
    for i in range(NSLOT):
        row = jnp.broadcast_to(slot_rank[:, i * LANES:(i + 1) * LANES], (8, LANES))
        row = jnp.where(lane < cap, row, jnp.where((lane == FLAG) & (most >= cap), -1.0, LATE))
        msg[i] = jnp.where(sub == i, row, LATE)
    seen[0] = msg[0]

    size = cap // PIECES

    def rows(u):
        i, p = UNITS[u]
        return pl.ds(i * cap + p * size, size)

    units = range(len(UNITS))
    first = {u: remote(send.at[pl.ds(i * cap + p * size, size)], blk.at[OWN + k, rows(u)], s1.at[u], r1.at[u], target(i))
             for u, (i, p) in enumerate(UNITS) if i}
    rank1 = [None] + [remote(msg.at[i], seen.at[i], sk.at[i], rk.at[i], target(i)) for i in range(1, NSLOT)]

    def route(kind, src, dst, to):
        return [remote(blk.at[src, rows(u)], blk.at[dst, rows(u)], sx.at[kind, u], rx.at[kind, u], to) for u in units], \
            remote(rks.at[src], rks.at[dst], sq.at[kind], rq.at[kind], to)

    to_left, rank_left = route(0, OWN + k, RIGHT + k, left)
    to_right, rank_right = route(1, OWN + k, LEFT + k, right)
    to_sib, rank_sib = route(2, OWN + k, OWN + k, sibling)
    to_inner, rank_inner = route(3, RIGHT + k, DIAG, inner)
    sib_right, rank_sib_right = route(4, RIGHT + k, RIGHT + k, sibling)
    sib_left, rank_sib_left = route(5, LEFT + k, LEFT + k, sibling)

    pl.semaphore_wait(barrier, len(partners))

    places = jnp.concatenate([pack[i * LANES:i * LANES + cap, :] for i in range(NSLOT)], axis=0)
    blk[OWN + k, 0:cap, :] = jnp.dot(places[0:cap], unit[...], preferred_element_type=jnp.float32).astype(jnp.bfloat16)
    for u in range(PIECES):
        for copies in (to_left, to_right, to_sib):
            copies[u].start()
    send[cap:, :] = jnp.dot(places[cap:], unit[...], preferred_element_type=jnp.float32).astype(jnp.bfloat16)
    for i in range(1, NSLOT):
        rank1[i].start()

    for u in units:
        if u in first:
            first[u].start()
    def spread(block):
        tile = rks[block]
        for j in range(n // LANES):
            line = jnp.full((8, LANES), LATE, jnp.float32)
            for i in range(NSLOT):
                start = i * cap - j * LANES
                if -cap < start < LANES:
                    piece = jnp.broadcast_to(tile[i:i + 1], (8, LANES))
                    if start % LANES:
                        piece = pltpu.roll(piece, start % LANES, 1)
                    line = jnp.where((lane >= start) & (lane < start + cap), piece, line)
            rcol[block, :, j * LANES:(j + 1) * LANES] = line
            rrow[block, j * LANES:(j + 1) * LANES, :] = jnp.broadcast_to(line[0:1], (LANES, LANES)).T

    def combine():
        for i in range(1, NSLOT):
            rank1[i].wait_recv()
        tile = seen[0]
        for i in range(1, NSLOT):
            tile = jnp.minimum(tile, seen[i])
        rks[OWN + k] = tile
        for copy in (rank_left, rank_right, rank_sib):
            copy.start()

    def relay(i):
        to_left[i].wait_recv()
        to_inner[i].start()
        sib_right[i].start()
        to_right[i].wait_recv()
        sib_left[i].start()

    for u in range(PIECES, len(UNITS)):
        first[u].wait_recv()
        for copies in (to_left, to_right, to_sib):
            copies[u].start()
        if u == RANKS:
            combine()
        if u == RANKS + 3:
            rank_left.wait_recv()
            rank_inner.start()
            rank_sib_right.start()
            rank_right.wait_recv()
            rank_sib_left.start()
        if u >= LAG:
            relay(u - LAG)

    def block_pair(row_block, col_block, start, width, row_start=0, row_count=n, both=True):
        span = pl.ds(row_start, row_count)
        score = lax.dot_general(blk[row_block, span, :], blk[col_block, start:start + width, :], (((1,), (1,)), ((), ())),
                                preferred_element_type=jnp.float32)
        row_rank, best = rrow[row_block, span, :], racc[row_block, span, :]
        for c in range(0, width, LANES):
            col = slice(start + c, start + c + LANES)
            part_score = score[:, c:c + LANES]
            keep = rcol[col_block, 0:1, col] < row_rank
            best = jnp.maximum(best, jnp.where(keep, part_score, -1.0))
            if both:
                rest = jnp.where(keep, -1.0, part_score).reshape(row_count // 8, 8, LANES)
                cacc[col_block, :, col] = jnp.maximum(cacc[col_block, :, col], jnp.max(rest, axis=0))
        racc[row_block, span, :] = best

    chunks = [(c, min(256, n - c)) for c in range(0, n, 256)]

    def covered(c, w):
        return 1 + max(u for u, (i, p) in enumerate(UNITS) if i * cap + p * size < c + w)

    racc[...] = jnp.full(racc.shape, -1.0, jnp.float32)
    cacc[...] = jnp.full(cacc.shape, -1.0, jnp.float32)
    spread(OWN + k)
    spread(RIGHT + k)
    for c, w in chunks:
        block_pair(OWN + k, OWN + k, c, w, both=False)

    rsib = {kind: [remote(blk.at[dst, rows(u)], blk.at[dst, rows(u)], sx.at[kind, u], rx.at[kind, u], sibling) for u in units]
            for kind, dst in ((2, OWN + o), (4, RIGHT + o), (5, LEFT + o))}
    rsib_rank = {kind: remote(rks.at[dst], rks.at[dst], sq.at[kind], rq.at[kind], sibling)
                 for kind, dst in ((2, OWN + o), (4, RIGHT + o), (5, LEFT + o))}
    rsib_rank[2].wait_recv()
    spread(OWN + o)
    for u in units:
        rsib[2][u].wait_recv()
    half = n // 2
    for c, w in chunks:
        block_pair(OWN, OWN + 1, c, w, row_start=pl.multiple_of(k * half, half), row_count=half)

    rank_inner.wait_recv()
    spread(DIAG)
    rsib_rank[4].wait_recv()
    spread(RIGHT + o)
    spread(LEFT + k)
    rsib_rank[5].wait_recv()
    spread(LEFT + o)

    def own_rows(col_block, c, w):
        def step(j, carry):
            block_pair(OWN + j, col_block, c, w)
            return carry
        lax.fori_loop(0, 2, step, 0)

    relayed, arrived = len(UNITS) - LAG, 0
    for c, w in chunks:
        while relayed < covered(c, w):
            relay(relayed)
            relayed += 1
        own_rows(RIGHT + k, c, w)
        if c + w < n:
            while arrived < covered(c, w):
                to_inner[arrived].wait_recv()
                arrived += 1
            own_rows(DIAG, c, w)
    for u in units:
        rsib[4][u].wait_recv()
        rsib[5][u].wait_recv()

    for c, w in chunks:
        block_pair(lsel, RIGHT + k, c, w)

    def side_rows(c, w):
        def step(j, carry):
            block_pair(jnp.where(j == 0, lsel, rsel), DIAG, c, w)
            return carry
        lax.fori_loop(0, 2, step, 0)

    for c, w in chunks:
        if c + w == n:
            while arrived < len(UNITS):
                to_inner[arrived].wait_recv()
                arrived += 1
            own_rows(DIAG, c, w)
        side_rows(c, w)

    heard = rks[0]
    for j in range(1, BLOCKS):
        heard = jnp.minimum(heard, rks[j])
    flagged = jnp.min(jnp.min(heard, axis=0, keepdims=True), axis=1, keepdims=True) < 0.0

    def folded(block):
        lines = []
        for j in range(n // LANES):
            span = slice(j * LANES, (j + 1) * LANES)
            by_row = jnp.max(racc[block, span, :].T, axis=0, keepdims=True)
            lines.append(jnp.broadcast_to(jnp.maximum(by_row, jnp.max(cacc[block, :, span], axis=0, keepdims=True)), (8, LANES)))
        tile = jnp.where((lane == FLAG) & flagged, 2.0, -1.0)
        for i in range(NSLOT):
            for j in range(n // LANES):
                start = j * LANES - i * cap
                if -LANES < start < cap:
                    piece = lines[j]
                    if start % LANES:
                        piece = pltpu.roll(piece, start % LANES, 1)
                    tile = jnp.where((sub == i) & (lane >= start) & (lane < min(cap, start + LANES)), piece, tile)
        return tile

    ends = ((OWN + o, sibling, sibling), (lsel, at(y, xor(k, x // 2), z, xm), left), (RIGHT + k, right, left),
            (rsel, at(y, xor(k, z % 2), z, xp), left), (DIAG, at(y, k, zin, xp), left))
    copies = []
    for j, (block, to, _) in enumerate(ends):
        part[j] = folded(block)
        copies.append(remote(part.at[j], rpart.at[j], sp.at[j], rp.at[j], to))
        copies[-1].start()
    best = folded(OWN + k)
    for j, copy in enumerate(copies):
        copy.wait_recv()
        best = jnp.maximum(best, rpart[j])
    fin[...] = best
    back = [None] + [remote(fin, home.at[i], sf.at[i], rf.at[i], source(i)) for i in range(1, NSLOT)]
    for i in range(1, NSLOT):
        back[i].start()
    home[0] = best

    for i in range(1, NSLOT):
        rank1[i].wait_send()
    for u in units:
        if u in first:
            first[u].wait_send()
        for group in (to_left, to_right, to_sib, to_inner, sib_right, sib_left):
            group[u].wait_send()
    for copy in (rank_left, rank_right, rank_sib, rank_inner, rank_sib_right, rank_sib_left, *copies):
        copy.wait_send()

    lines = []
    for i in range(NSLOT):
        if i:
            back[i].wait_recv()
        value = home[i, i:i + 1, :]
        high = value.astype(jnp.bfloat16).astype(jnp.float32)
        middle = (value - high).astype(jnp.bfloat16).astype(jnp.float32)
        low = value - high - middle
        lines.append(jnp.where(sub == 0, high, jnp.where(sub == 1, middle, jnp.where(sub == 2, low, 0.0))).astype(jnp.bfloat16))
    picked = jnp.dot(jnp.concatenate(lines, axis=1), pack[...], preferred_element_type=jnp.float32)
    result = picked[0:1] + picked[1:2] + picked[2:3]
    over = jnp.max(best[0:1, FLAG:], axis=1, keepdims=True)
    out_ref[...] = jnp.concatenate([result, jnp.broadcast_to(over, (1, LANES))], axis=1).reshape(DOC + LANES)
    for i in range(1, NSLOT):
        back[i].wait_send()


def nearest(cap, number, embeddings, routes, ranks):
    n = NSLOT * cap
    f32, bf16 = jnp.float32, jnp.bfloat16
    dma = pltpu.SemaphoreType.DMA
    vmem = pl.BlockSpec(memory_space=pltpu.VMEM)
    return pl.pallas_call(
        lambda *refs: kernel(cap, *refs),
        out_shape=jax.ShapeDtypeStruct((DOC + LANES,), f32),
        in_specs=[vmem] * 3,
        out_specs=vmem,
        scratch_shapes=[
            pltpu.VMEM((DOC, D), bf16),
            pltpu.VMEM((NSLOT * LANES, DOC), bf16),
            pltpu.VMEM((n, D), bf16),
            pltpu.VMEM((NSLOT, 8, LANES), f32),
            pltpu.VMEM((NSLOT, 8, LANES), f32),
            pltpu.VMEM((BLOCKS, n, D), bf16),
            pltpu.VMEM((BLOCKS, 8, LANES), f32),
            pltpu.VMEM((BLOCKS, 8, n), f32),
            pltpu.VMEM((BLOCKS, n, LANES), f32),
            pltpu.VMEM((BLOCKS, n, LANES), f32),
            pltpu.VMEM((BLOCKS, 8, n), f32),
            pltpu.VMEM((5, 8, LANES), f32),
            pltpu.VMEM((5, 8, LANES), f32),
            pltpu.VMEM((8, LANES), f32),
            pltpu.VMEM((NSLOT, 8, LANES), f32),
            dma((len(UNITS),)), dma((len(UNITS),)), dma((NSLOT,)), dma((NSLOT,)),
            dma((6, len(UNITS))), dma((6, len(UNITS))), dma((6,)), dma((6,)),
            dma((5,)), dma((5,)), dma((NSLOT,)), dma((NSLOT,)),
        ],
        compiler_params=pltpu.CompilerParams(collective_id=number, has_side_effects=True, vmem_limit_bytes=56 * 2**20),
        cost_estimate=pl.CostEstimate(flops=17 * n * n * D, bytes_accessed=2 * DOC * D, transcendentals=DOC),
    )(embeddings, routes.reshape(1, DOC), ranks)


def body(embeddings, routes, ranks):
    quick = nearest(64, 1, embeddings, routes, ranks)
    return lax.cond(quick[DOC] > 1.5, lambda: nearest(96, 2, embeddings, routes, ranks)[:DOC], lambda: quick[:DOC])


def solution(mesh):
    in_specs = (P(("grp", "blk"), None), P(("grp", "blk"), None), P(("grp", "blk")))
    return jax.shard_map(body, mesh=mesh, in_specs=in_specs, out_specs=P(("grp", "blk")), check_vma=False)
```

```python
import jax
import jax.numpy as jnp
from jax import lax
from jax.experimental import pallas as pl
from jax.experimental.pallas import tpu as pltpu
from jax.sharding import PartitionSpec as P

MESH = pl.DeviceIdType.MESH
D = 1024
DOC = 384
NSLOT = 8
LANES = 128
LATE = float(1 << 20)
DY = (0, 0, 1, 3, 1, 3, 2, 2)
ZZ = (0, 1, 0, 0, 1, 1, 0, 1)
OWN, LEFT, RIGHT, DIAG, BLOCKS = 0, 2, 4, 6, 7
GROUPS = ((0,), (1, 2, 3, 6), (7, 4, 5))
PIECES = 2
LAG = 4
RANKS = 10
UNITS = tuple((i, p) for group in GROUPS for p in range(PIECES) for i in group)
FLAG = LANES - 1


def xor(a, b):
    return a + b - 2 * a * b


def kernel(cap, emb_ref, route_ref, rank_ref, out_ref, flag_ref, unit, pack, send, msg, seen, blk, rks, rcol, rrow, racc, cacc,
           part, rpart, fin, home, s1, r1, sk, rk, sx, rx, sq, rq, sp, rp, sf, rf, se):
    n = NSLOT * cap
    g, b = lax.axis_index("grp"), lax.axis_index("blk")
    y, k, z, x = g // 2, g % 2, b // 4, b % 4
    o = 1 - k
    zin, zout = z + 1 - 2 * (z % 2), 3 - z
    xp, xm = (x + 1) % 4, (x + 3) % 4
    lsel, rsel = LEFT + xor(k, x // 2), RIGHT + xor(k, z % 2)

    def at(yy, kk, zz, xx):
        return (yy * 2 + kk, zz * 4 + xx)

    def target(i):
        return at((y + DY[i]) % 4, k, zout if ZZ[i] else z, x)

    def source(i):
        return at((y + 4 - DY[i]) % 4, k, zout if ZZ[i] else z, x)

    left, right, sibling, inner = at(y, k, z, xm), at(y, k, z, xp), at(y, o, z, x), at(y, k, zin, x)

    def remote(src, dst, ss, rs, to):
        return pltpu.make_async_remote_copy(src_ref=src, dst_ref=dst, send_sem=ss, recv_sem=rs, device_id=to, device_id_type=MESH)

    load = pltpu.make_async_copy(emb_ref, unit, se)
    load.start()
    barrier = pltpu.get_barrier_semaphore()
    partners = [target(i) for i in range(1, NSLOT)] + [left, right, sibling, inner]
    partners += [at(y, o, z, xm), at(y, o, z, xp), at(y, k, zin, xm), at(y, k, zin, xp)]
    for to in partners:
        pl.semaphore_signal(barrier, inc=1, device_id=to, device_id_type=MESH)

    load.wait()
    values = unit[...].astype(jnp.float32)
    unit[...] = (values * lax.rsqrt(jnp.sum(values * values, axis=1, keepdims=True) + 1e-06)).astype(jnp.bfloat16)
    cluster = route_ref[...] // 16
    index = jnp.zeros((1, DOC), jnp.int32)
    for i in range(1, NSLOT):
        zz = zout if ZZ[i] else z
        index = jnp.where(cluster == ((y + DY[i]) % 4) * 2 + zz // 2, i, index)
    chosen = index == lax.broadcasted_iota(jnp.int32, (NSLOT, DOC), 0)
    onehot = jnp.where(chosen, 1.0, 0.0)
    before = lax.broadcasted_iota(jnp.int32, (DOC, DOC), 0) < lax.broadcasted_iota(jnp.int32, (DOC, DOC), 1)
    counts = jnp.dot(onehot.astype(jnp.bfloat16), jnp.where(before, 1.0, 0.0).astype(jnp.bfloat16),
                     preferred_element_type=jnp.float32)
    position = jnp.sum(counts * onehot, axis=0, keepdims=True).astype(jnp.int32)
    place = index * LANES + position
    most = jnp.max(position, axis=1, keepdims=True)
    for i in range(NSLOT):
        hit = place == lax.broadcasted_iota(jnp.int32, (LANES, DOC), 0) + i * LANES
        pack[i * LANES:(i + 1) * LANES, :] = jnp.where(hit, 1.0, 0.0).astype(jnp.bfloat16)

    rank = rank_ref[...].reshape(1, DOC)
    line = lax.broadcasted_iota(jnp.int32, (8, DOC), 0)
    digits = jnp.where(line == 0, rank // 256, jnp.where(line == 1, rank % 256, 1)).astype(jnp.float32).astype(jnp.bfloat16)
    placed = lax.dot_general(digits, pack[...], (((1,), (1,)), ((), ())), preferred_element_type=jnp.float32)
    slot_rank = placed[0:1] * 256.0 + placed[1:2] + (1.0 - placed[2:3]) * LATE
    sub, lane = lax.broadcasted_iota(jnp.int32, (8, LANES), 0), lax.broadcasted_iota(jnp.int32, (8, LANES), 1)
    for i in range(NSLOT):
        row = jnp.broadcast_to(slot_rank[:, i * LANES:(i + 1) * LANES], (8, LANES))
        row = jnp.where(lane < cap, row, jnp.where((lane == FLAG) & (most >= cap), -1.0, LATE))
        msg[i] = jnp.where(sub == i, row, LATE)
    seen[0] = msg[0]

    size = cap // PIECES

    def rows(u):
        i, p = UNITS[u]
        return pl.ds(i * cap + p * size, size)

    units = range(len(UNITS))
    first = {u: remote(send.at[pl.ds(i * cap + p * size, size)], blk.at[OWN + k, rows(u)], s1.at[u], r1.at[u], target(i))
             for u, (i, p) in enumerate(UNITS) if i}
    rank1 = [None] + [remote(msg.at[i], seen.at[i], sk.at[i], rk.at[i], target(i)) for i in range(1, NSLOT)]

    def route(kind, src, dst, to):
        return [remote(blk.at[src, rows(u)], blk.at[dst, rows(u)], sx.at[kind, u], rx.at[kind, u], to) for u in units], \
            remote(rks.at[src], rks.at[dst], sq.at[kind], rq.at[kind], to)

    to_left, rank_left = route(0, OWN + k, RIGHT + k, left)
    to_right, rank_right = route(1, OWN + k, LEFT + k, right)
    to_sib, rank_sib = route(2, OWN + k, OWN + k, sibling)
    to_inner, rank_inner = route(3, RIGHT + k, DIAG, inner)
    sib_right, rank_sib_right = route(4, RIGHT + k, RIGHT + k, sibling)
    sib_left, rank_sib_left = route(5, LEFT + k, LEFT + k, sibling)

    pl.semaphore_wait(barrier, len(partners))

    places = jnp.concatenate([pack[i * LANES:i * LANES + cap, :] for i in range(NSLOT)], axis=0)
    blk[OWN + k, 0:cap, :] = jnp.dot(places[0:cap], unit[...], preferred_element_type=jnp.float32).astype(jnp.bfloat16)
    for u in range(PIECES):
        remote(blk.at[OWN + k, rows(u)], blk.at[DIAG, rows(u)], sx.at[3, u], rx.at[3, u], at(y, k, zin, xm)).start()
        to_right[u].start()
        to_sib[u].start()
    send[cap:, :] = jnp.dot(places[cap:], unit[...], preferred_element_type=jnp.float32).astype(jnp.bfloat16)
    for i in range(1, NSLOT):
        rank1[i].start()

    for u in units:
        if u in first:
            first[u].start()
    def spread(block):
        tile = rks[block]
        for j in range(n // LANES):
            line = jnp.full((8, LANES), LATE, jnp.float32)
            for i in range(NSLOT):
                start = i * cap - j * LANES
                if -cap < start < LANES:
                    piece = jnp.broadcast_to(tile[i:i + 1], (8, LANES))
                    if start % LANES:
                        piece = pltpu.roll(piece, start % LANES, 1)
                    line = jnp.where((lane >= start) & (lane < start + cap), piece, line)
            rcol[block, :, j * LANES:(j + 1) * LANES] = line
            rrow[block, j * LANES:(j + 1) * LANES, :] = jnp.broadcast_to(line[0:1], (LANES, LANES)).T

    def combine():
        for i in range(1, NSLOT):
            rank1[i].wait_recv()
        tile = seen[0]
        for i in range(1, NSLOT):
            tile = jnp.minimum(tile, seen[i])
        rks[OWN + k] = tile
        for copy in (rank_left, rank_right, rank_sib):
            copy.start()

    def relay(u):
        if u >= PIECES:
            to_left[u].wait_recv()
            to_inner[u].start()
            sib_right[u].start()
        to_right[u].wait_recv()
        sib_left[u].start()

    for u in range(PIECES, len(UNITS)):
        first[u].wait_recv()
        for copies in (to_left, to_right, to_sib):
            copies[u].start()
        if u == RANKS:
            combine()
        if u == RANKS + 3:
            rank_left.wait_recv()
            rank_inner.start()
            rank_sib_right.start()
            rank_right.wait_recv()
            rank_sib_left.start()
        if u >= LAG:
            relay(u - LAG)

    def many_rows(row_blocks, col_block, start, width):
        lines = [cacc[col_block, :, start + c:start + c + LANES] for c in range(0, width, LANES)]
        for row_block in row_blocks:
            score = lax.dot_general(blk[row_block], blk[col_block, start:start + width, :], (((1,), (1,)), ((), ())),
                                    preferred_element_type=jnp.float32)
            row_rank, best = rrow[row_block], racc[row_block]
            for j, c in enumerate(range(0, width, LANES)):
                part_score = score[:, c:c + LANES]
                keep = rcol[col_block, 0:1, start + c:start + c + LANES] < row_rank
                best = jnp.maximum(best, jnp.where(keep, part_score, -1.0))
                rest = jnp.where(keep, -1.0, part_score).reshape(n // 8, 8, LANES)
                lines[j] = jnp.maximum(lines[j], jnp.max(rest, axis=0))
            racc[row_block] = best
        for j, c in enumerate(range(0, width, LANES)):
            cacc[col_block, :, start + c:start + c + LANES] = lines[j]

    def block_pair(row_block, col_block, start, width, row_start=0, row_count=n, both=True):
        span = pl.ds(row_start, row_count)
        score = lax.dot_general(blk[row_block, span, :], blk[col_block, start:start + width, :], (((1,), (1,)), ((), ())),
                                preferred_element_type=jnp.float32)
        row_rank, best = rrow[row_block, span, :], racc[row_block, span, :]
        for c in range(0, width, LANES):
            col = slice(start + c, start + c + LANES)
            part_score = score[:, c:c + LANES]
            keep = rcol[col_block, 0:1, col] < row_rank
            best = jnp.maximum(best, jnp.where(keep, part_score, -1.0))
            if both:
                rest = jnp.where(keep, -1.0, part_score).reshape(row_count // 8, 8, LANES)
                cacc[col_block, :, col] = jnp.maximum(cacc[col_block, :, col], jnp.max(rest, axis=0))
        racc[row_block, span, :] = best

    chunks = [(c, min(256, n - c)) for c in range(0, n, 256)]

    def covered(c, w):
        return 1 + max(u for u, (i, p) in enumerate(UNITS) if i * cap + p * size < c + w)

    for u in range(PIECES):
        to_left[u].start()

    rsib = {kind: [remote(blk.at[dst, rows(u)], blk.at[dst, rows(u)], sx.at[kind, u], rx.at[kind, u], sibling) for u in units]
            for kind, dst in ((2, OWN + o), (4, RIGHT + o), (5, LEFT + o))}
    rsib_rank = {kind: remote(rks.at[dst], rks.at[dst], sq.at[kind], rq.at[kind], sibling)
                 for kind, dst in ((2, OWN + o), (4, RIGHT + o), (5, LEFT + o))}

    def own_rows(col_block, c, w):
        many_rows((OWN, OWN + 1), col_block, c, w)

    relays = list(range(len(UNITS) - LAG, len(UNITS)))

    def relay_next():
        if relays:
            relay(relays.pop(0))

    racc[...] = jnp.full(racc.shape, -1.0, jnp.float32)
    cacc[...] = jnp.full(cacc.shape, -1.0, jnp.float32)
    spread(OWN + k)
    for c, w in chunks:
        relay_next()
        block_pair(OWN + k, OWN + k, c, w, both=False)
    rsib_rank[2].wait_recv()
    spread(OWN + o)
    relay_next()
    for u in units:
        rsib[2][u].wait_recv()
    half = n // 2
    for c, w in chunks:
        block_pair(OWN, OWN + 1, c, w, row_start=pl.multiple_of(k * half, half), row_count=half)
    while relays:
        relay_next()
    rank_inner.wait_recv()
    spread(DIAG)
    early = covered(*chunks[0])
    for u in range(early):
        to_inner[u].wait_recv()
    own_rows(DIAG, *chunks[0])
    spread(RIGHT + k)
    for c, w in chunks[1:]:
        own_rows(RIGHT + k, c, w)
    spread(LEFT + k)
    rsib_rank[5].wait_recv()
    spread(LEFT + o)
    rsib_rank[4].wait_recv()
    spread(RIGHT + o)
    for u in units:
        rsib[5][u].wait_recv()
    for c, w in chunks[1:]:
        block_pair(lsel, RIGHT + k, c, w)
    for u in range(PIECES):
        to_left[u].wait_recv()
        sib_right[u].start()
    own_rows(RIGHT + k, *chunks[0])
    block_pair(lsel, RIGHT + k, *chunks[0])
    for u in units:
        rsib[4][u].wait_recv()

    def side_rows(c, w):
        many_rows((lsel, rsel), DIAG, c, w)

    side_rows(*chunks[0])
    for u in units[early:]:
        to_inner[u].wait_recv()
    for c, w in chunks[1:]:
        many_rows((OWN, OWN + 1, lsel, rsel), DIAG, c, w)

    heard = rks[0]
    for j in range(1, BLOCKS):
        heard = jnp.minimum(heard, rks[j])
    flagged = jnp.min(jnp.min(heard, axis=0, keepdims=True), axis=1, keepdims=True) < 0.0

    def folded(block):
        lines = []
        for j in range(n // LANES):
            span = slice(j * LANES, (j + 1) * LANES)
            by_row = jnp.max(racc[block, span, :].T, axis=0, keepdims=True)
            lines.append(jnp.broadcast_to(jnp.maximum(by_row, jnp.max(cacc[block, :, span], axis=0, keepdims=True)), (8, LANES)))
        tile = jnp.where((lane == FLAG) & flagged, 2.0, -1.0)
        for i in range(NSLOT):
            for j in range(n // LANES):
                start = j * LANES - i * cap
                if -LANES < start < cap:
                    piece = lines[j]
                    if start % LANES:
                        piece = pltpu.roll(piece, start % LANES, 1)
                    tile = jnp.where((sub == i) & (lane >= start) & (lane < min(cap, start + LANES)), piece, tile)
        return tile

    ends = ((OWN + o, sibling, sibling), (lsel, at(y, xor(k, x // 2), z, xm), left), (RIGHT + k, right, left),
            (rsel, at(y, xor(k, z % 2), z, xp), left), (DIAG, at(y, k, zin, xp), left))
    copies = []
    for j, (block, to, _) in enumerate(ends):
        part[j] = folded(block)
        copies.append(remote(part.at[j], rpart.at[j], sp.at[j], rp.at[j], to))
        copies[-1].start()
    best = folded(OWN + k)
    for j, copy in enumerate(copies):
        copy.wait_recv()
        best = jnp.maximum(best, rpart[j])
    fin[...] = best
    back = [None] + [remote(fin, home.at[i], sf.at[i], rf.at[i], source(i)) for i in range(1, NSLOT)]
    for i in range(1, NSLOT):
        back[i].start()
    home[0] = best

    for i in range(1, NSLOT):
        rank1[i].wait_send()
    for u in units:
        if u in first:
            first[u].wait_send()
        for group in (to_left, to_right, to_sib, to_inner, sib_right, sib_left):
            group[u].wait_send()
    for copy in (rank_left, rank_right, rank_sib, rank_inner, rank_sib_right, rank_sib_left, *copies):
        copy.wait_send()

    lines = []
    for i in range(NSLOT):
        if i:
            back[i].wait_recv()
        value = home[i, i:i + 1, :]
        high = value.astype(jnp.bfloat16).astype(jnp.float32)
        middle = (value - high).astype(jnp.bfloat16).astype(jnp.float32)
        low = value - high - middle
        lines.append(jnp.where(sub == 0, high, jnp.where(sub == 1, middle, jnp.where(sub == 2, low, 0.0))).astype(jnp.bfloat16))
    picked = jnp.dot(jnp.concatenate(lines, axis=1), pack[...], preferred_element_type=jnp.float32)
    result = picked[0:1] + picked[1:2] + picked[2:3]
    over = jnp.max(best[0:1, FLAG:], axis=1, keepdims=True)
    out_ref[...] = result.reshape(DOC)
    flag_ref[...] = jnp.broadcast_to(over, (1, LANES)).reshape(LANES)
    for i in range(1, NSLOT):
        back[i].wait_send()


def nearest(cap, number, embeddings, routes, ranks):
    n = NSLOT * cap
    f32, bf16 = jnp.float32, jnp.bfloat16
    dma = pltpu.SemaphoreType.DMA
    vmem = pl.BlockSpec(memory_space=pltpu.VMEM)
    return pl.pallas_call(
        lambda *refs: kernel(cap, *refs),
        out_shape=[jax.ShapeDtypeStruct((DOC,), f32), jax.ShapeDtypeStruct((LANES,), f32)],
        in_specs=[pl.BlockSpec(memory_space=pl.ANY), vmem, vmem],
        out_specs=[vmem, vmem],
        scratch_shapes=[
            pltpu.VMEM((DOC, D), bf16),
            pltpu.VMEM((NSLOT * LANES, DOC), bf16),
            pltpu.VMEM((n, D), bf16),
            pltpu.VMEM((NSLOT, 8, LANES), f32),
            pltpu.VMEM((NSLOT, 8, LANES), f32),
            pltpu.VMEM((BLOCKS, n, D), bf16),
            pltpu.VMEM((BLOCKS, 8, LANES), f32),
            pltpu.VMEM((BLOCKS, 8, n), f32),
            pltpu.VMEM((BLOCKS, n, LANES), f32),
            pltpu.VMEM((BLOCKS, n, LANES), f32),
            pltpu.VMEM((BLOCKS, 8, n), f32),
            pltpu.VMEM((5, 8, LANES), f32),
            pltpu.VMEM((5, 8, LANES), f32),
            pltpu.VMEM((8, LANES), f32),
            pltpu.VMEM((NSLOT, 8, LANES), f32),
            dma((len(UNITS),)), dma((len(UNITS),)), dma((NSLOT,)), dma((NSLOT,)),
            dma((6, len(UNITS))), dma((6, len(UNITS))), dma((6,)), dma((6,)),
            dma((5,)), dma((5,)), dma((NSLOT,)), dma((NSLOT,)), dma,
        ],
        compiler_params=pltpu.CompilerParams(collective_id=number, has_side_effects=True, vmem_limit_bytes=56 * 2**20),
        cost_estimate=pl.CostEstimate(flops=17 * n * n * D, bytes_accessed=2 * DOC * D, transcendentals=DOC),
    )(embeddings, routes.reshape(1, DOC), ranks)


def body(embeddings, routes, ranks):
    quick, flag = nearest(64, 1, embeddings, routes, ranks)
    return lax.cond(flag[0] > 1.5, lambda: nearest(96, 2, embeddings, routes, ranks)[0], lambda: quick)


def solution(mesh):
    in_specs = (P(("grp", "blk"), None), P(("grp", "blk"), None), P(("grp", "blk")))
    return jax.shard_map(body, mesh=mesh, in_specs=in_specs, out_specs=P(("grp", "blk")), check_vma=False)
```

```python
import jax
import jax.numpy as jnp
from jax import lax
from jax.experimental import pallas as pl
from jax.experimental.pallas import tpu as pltpu
from jax.sharding import PartitionSpec as P

MESH = pl.DeviceIdType.MESH
D = 1024
DOC = 384
NSLOT = 8
LANES = 128
LATE = float(1 << 20)
DY = (0, 0, 1, 3, 1, 3, 2, 2)
ZZ = (0, 1, 0, 0, 1, 1, 0, 1)
OWN, LEFT, RIGHT, DIAG, BLOCKS = 0, 2, 4, 6, 7
GROUPS = ((0,), (1, 2, 3, 6), (7, 5, 4))
PIECES = 2
LAG = 5
RANKS = 10
UNITS = tuple((i, p) for group in GROUPS for p in range(PIECES) for i in group)
FLAG = LANES - 1


def xor(a, b):
    return a + b - 2 * a * b


def kernel(cap, emb_ref, route_ref, rank_ref, out_ref, flag_ref, routed, ranked, unit, pack, send, msg, seen, blk, rks, rcol, rrow, racc, cacc,
           part, rpart, fin, home, s1, r1, sk, rk, sx, rx, sq, rq, sp, rp, sf, rf, se):
    n = NSLOT * cap
    g, b = lax.axis_index("grp"), lax.axis_index("blk")
    y, k, z, x = g // 2, g % 2, b // 4, b % 4
    o = 1 - k
    zin, zout = z + 1 - 2 * (z % 2), 3 - z
    xp, xm = (x + 1) % 4, (x + 3) % 4
    lsel, rsel = LEFT + xor(k, x // 2), RIGHT + xor(k, z % 2)

    def at(yy, kk, zz, xx):
        return (yy * 2 + kk, zz * 4 + xx)

    def target(i):
        return at((y + DY[i]) % 4, k, zout if ZZ[i] else z, x)

    def source(i):
        return at((y + 4 - DY[i]) % 4, k, zout if ZZ[i] else z, x)

    left, right, sibling, inner = at(y, k, z, xm), at(y, k, z, xp), at(y, o, z, x), at(y, k, zin, x)

    def remote(src, dst, ss, rs, to):
        return pltpu.make_async_remote_copy(src_ref=src, dst_ref=dst, send_sem=ss, recv_sem=rs, device_id=to, device_id_type=MESH)

    loads = [pltpu.make_async_copy(src, dst, se.at[j]) for j, (src, dst) in enumerate(((route_ref, routed), (rank_ref, ranked), (emb_ref, unit)))]
    for load in loads:
        load.start()
    barrier = pltpu.get_barrier_semaphore()
    partners = [target(i) for i in range(1, NSLOT)] + [left, right, sibling, inner]
    partners += [at(y, o, z, xm), at(y, o, z, xp), at(y, k, zin, xm), at(y, k, zin, xp)]
    for to in partners:
        pl.semaphore_signal(barrier, inc=1, device_id=to, device_id_type=MESH)

    loads[0].wait()
    cluster = routed[...] // 16
    index = jnp.zeros((1, DOC), jnp.int32)
    for i in range(1, NSLOT):
        zz = zout if ZZ[i] else z
        index = jnp.where(cluster == ((y + DY[i]) % 4) * 2 + zz // 2, i, index)
    chosen = index == lax.broadcasted_iota(jnp.int32, (NSLOT, DOC), 0)
    onehot = jnp.where(chosen, 1.0, 0.0)
    before = lax.broadcasted_iota(jnp.int32, (DOC, DOC), 0) < lax.broadcasted_iota(jnp.int32, (DOC, DOC), 1)
    counts = jnp.dot(onehot.astype(jnp.bfloat16), jnp.where(before, 1.0, 0.0).astype(jnp.bfloat16),
                     preferred_element_type=jnp.float32)
    position = jnp.sum(counts * onehot, axis=0, keepdims=True).astype(jnp.int32)
    place = index * LANES + position
    most = jnp.max(position, axis=1, keepdims=True)
    for i in range(NSLOT):
        hit = place == lax.broadcasted_iota(jnp.int32, (LANES, DOC), 0) + i * LANES
        pack[i * LANES:(i + 1) * LANES, :] = jnp.where(hit, 1.0, 0.0).astype(jnp.bfloat16)

    loads[1].wait()
    rank = ranked[...].reshape(1, DOC)
    line = lax.broadcasted_iota(jnp.int32, (8, DOC), 0)
    digits = jnp.where(line == 0, rank // 256, jnp.where(line == 1, rank % 256, 1)).astype(jnp.float32).astype(jnp.bfloat16)
    placed = lax.dot_general(digits, pack[...], (((1,), (1,)), ((), ())), preferred_element_type=jnp.float32)
    slot_rank = placed[0:1] * 256.0 + placed[1:2] + (1.0 - placed[2:3]) * LATE
    sub, lane = lax.broadcasted_iota(jnp.int32, (8, LANES), 0), lax.broadcasted_iota(jnp.int32, (8, LANES), 1)
    for i in range(NSLOT):
        row = jnp.broadcast_to(slot_rank[:, i * LANES:(i + 1) * LANES], (8, LANES))
        row = jnp.where(lane < cap, row, jnp.where((lane == FLAG) & (most >= cap), -1.0, LATE))
        msg[i] = jnp.where(sub == i, row, LATE)
    seen[0] = msg[0]

    size = cap // PIECES

    loads[2].wait()
    values = unit[...].astype(jnp.float32)
    unit[...] = (values * lax.rsqrt(jnp.sum(values * values, axis=1, keepdims=True) + 1e-06)).astype(jnp.bfloat16)

    def rows(u):
        i, p = UNITS[u]
        return pl.ds(i * cap + p * size, size)

    units = range(len(UNITS))
    first = {u: remote(send.at[pl.ds(i * cap + p * size, size)], blk.at[OWN + k, rows(u)], s1.at[u], r1.at[u], target(i))
             for u, (i, p) in enumerate(UNITS) if i}
    rank1 = [None] + [remote(msg.at[i], seen.at[i], sk.at[i], rk.at[i], target(i)) for i in range(1, NSLOT)]

    def route(kind, src, dst, to):
        return [remote(blk.at[src, rows(u)], blk.at[dst, rows(u)], sx.at[kind, u], rx.at[kind, u], to) for u in units], \
            remote(rks.at[src], rks.at[dst], sq.at[kind], rq.at[kind], to)

    to_left, rank_left = route(0, OWN + k, RIGHT + k, left)
    to_right, rank_right = route(1, OWN + k, LEFT + k, right)
    to_sib, rank_sib = route(2, OWN + k, OWN + k, sibling)
    to_inner, rank_inner = route(3, RIGHT + k, DIAG, inner)
    sib_right, rank_sib_right = route(4, RIGHT + k, RIGHT + k, sibling)
    sib_left, rank_sib_left = route(5, LEFT + k, LEFT + k, sibling)

    pl.semaphore_wait(barrier, len(partners))

    places = jnp.concatenate([pack[i * LANES:i * LANES + cap, :] for i in range(NSLOT)], axis=0)
    blk[OWN + k, 0:cap, :] = jnp.dot(places[0:cap], unit[...], preferred_element_type=jnp.float32).astype(jnp.bfloat16)
    for u in range(PIECES):
        remote(blk.at[OWN + k, rows(u)], blk.at[DIAG, rows(u)], sx.at[3, u], rx.at[3, u], at(y, k, zin, xm)).start()
        to_right[u].start()
        to_sib[u].start()
    send[cap:, :] = jnp.dot(places[cap:], unit[...], preferred_element_type=jnp.float32).astype(jnp.bfloat16)
    for i in range(1, NSLOT):
        rank1[i].start()

    for u in units:
        if u in first:
            first[u].start()
    def spread(block):
        tile = rks[block]
        for j in range(n // LANES):
            line = jnp.full((8, LANES), LATE, jnp.float32)
            for i in range(NSLOT):
                start = i * cap - j * LANES
                if -cap < start < LANES:
                    piece = jnp.broadcast_to(tile[i:i + 1], (8, LANES))
                    if start % LANES:
                        piece = pltpu.roll(piece, start % LANES, 1)
                    line = jnp.where((lane >= start) & (lane < start + cap), piece, line)
            rcol[block, :, j * LANES:(j + 1) * LANES] = line
            rrow[block, j * LANES:(j + 1) * LANES, :] = jnp.broadcast_to(line[0:1], (LANES, LANES)).T

    def combine():
        for i in range(1, NSLOT):
            rank1[i].wait_recv()
        tile = seen[0]
        for i in range(1, NSLOT):
            tile = jnp.minimum(tile, seen[i])
        rks[OWN + k] = tile
        for copy in (rank_left, rank_right, rank_sib):
            copy.start()

    def relay(u):
        if u >= PIECES:
            to_left[u].wait_recv()
            to_inner[u].start()
            sib_right[u].start()
        to_right[u].wait_recv()
        sib_left[u].start()

    for u in range(PIECES, len(UNITS)):
        first[u].wait_recv()
        for copies in (to_left, to_right, to_sib):
            copies[u].start()
        if u == RANKS:
            combine()
        if u == RANKS + 3:
            rank_left.wait_recv()
            rank_inner.start()
            rank_sib_right.start()
            rank_right.wait_recv()
            rank_sib_left.start()
        if u >= LAG:
            relay(u - LAG)

    def many_rows(row_blocks, col_block, start, width):
        lines = [cacc[col_block, :, start + c:start + c + LANES] for c in range(0, width, LANES)]
        for row_block in row_blocks:
            score = lax.dot_general(blk[row_block], blk[col_block, start:start + width, :], (((1,), (1,)), ((), ())),
                                    preferred_element_type=jnp.float32)
            row_rank, best = rrow[row_block], racc[row_block]
            for j, c in enumerate(range(0, width, LANES)):
                part_score = score[:, c:c + LANES]
                keep = rcol[col_block, 0:1, start + c:start + c + LANES] < row_rank
                best = jnp.maximum(best, jnp.where(keep, part_score, -1.0))
                rest = jnp.where(keep, -1.0, part_score).reshape(n // 8, 8, LANES)
                lines[j] = jnp.maximum(lines[j], jnp.max(rest, axis=0))
            racc[row_block] = best
        for j, c in enumerate(range(0, width, LANES)):
            cacc[col_block, :, start + c:start + c + LANES] = lines[j]

    def block_pair(row_block, col_block, start, width, row_start=0, row_count=n, both=True):
        span = pl.ds(row_start, row_count)
        score = lax.dot_general(blk[row_block, span, :], blk[col_block, start:start + width, :], (((1,), (1,)), ((), ())),
                                preferred_element_type=jnp.float32)
        row_rank, best = rrow[row_block, span, :], racc[row_block, span, :]
        for c in range(0, width, LANES):
            col = slice(start + c, start + c + LANES)
            part_score = score[:, c:c + LANES]
            keep = rcol[col_block, 0:1, col] < row_rank
            best = jnp.maximum(best, jnp.where(keep, part_score, -1.0))
            if both:
                rest = jnp.where(keep, -1.0, part_score).reshape(row_count // 8, 8, LANES)
                cacc[col_block, :, col] = jnp.maximum(cacc[col_block, :, col], jnp.max(rest, axis=0))
        racc[row_block, span, :] = best

    chunks = [(c, min(256, n - c)) for c in range(0, n, 256)]

    def covered(c, w):
        return 1 + max(u for u, (i, p) in enumerate(UNITS) if i * cap + p * size < c + w)

    for u in range(PIECES):
        to_left[u].start()

    rsib = {kind: [remote(blk.at[dst, rows(u)], blk.at[dst, rows(u)], sx.at[kind, u], rx.at[kind, u], sibling) for u in units]
            for kind, dst in ((2, OWN + o), (4, RIGHT + o), (5, LEFT + o))}
    rsib_rank = {kind: remote(rks.at[dst], rks.at[dst], sq.at[kind], rq.at[kind], sibling)
                 for kind, dst in ((2, OWN + o), (4, RIGHT + o), (5, LEFT + o))}

    def own_rows(col_block, c, w):
        many_rows((OWN, OWN + 1), col_block, c, w)

    relays = list(range(len(UNITS) - LAG, len(UNITS)))

    def relay_next():
        if relays:
            relay(relays.pop(0))

    racc[...] = jnp.full(racc.shape, -1.0, jnp.float32)
    cacc[...] = jnp.full(cacc.shape, -1.0, jnp.float32)
    spread(OWN + k)
    for c, w in chunks:
        relay_next()
        block_pair(OWN + k, OWN + k, c, w, both=False)
    rsib_rank[2].wait_recv()
    spread(OWN + o)
    relay_next()
    for u in units:
        rsib[2][u].wait_recv()
    half = n // 2
    for c, w in chunks:
        block_pair(OWN, OWN + 1, c, w, row_start=pl.multiple_of(k * half, half), row_count=half)
    while relays:
        relay_next()
    rank_inner.wait_recv()
    spread(DIAG)
    early = covered(*chunks[0])
    for u in range(early):
        to_inner[u].wait_recv()
    own_rows(DIAG, *chunks[0])
    spread(RIGHT + k)
    for c, w in chunks[1:]:
        own_rows(RIGHT + k, c, w)
    spread(LEFT + k)
    rsib_rank[5].wait_recv()
    spread(LEFT + o)
    rsib_rank[4].wait_recv()
    spread(RIGHT + o)
    for u in range(PIECES):
        to_left[u].wait_recv()
        sib_right[u].start()
    own_rows(RIGHT + k, *chunks[0])
    for u in units:
        rsib[5][u].wait_recv()
    for c, w in chunks[1:]:
        block_pair(lsel, RIGHT + k, c, w)
    block_pair(lsel, RIGHT + k, *chunks[0])
    for u in units:
        rsib[4][u].wait_recv()

    def side_rows(c, w):
        many_rows((lsel, rsel), DIAG, c, w)

    side_rows(*chunks[0])
    for u in units[early:]:
        to_inner[u].wait_recv()
    for c, w in chunks[1:]:
        many_rows((OWN, OWN + 1, lsel, rsel), DIAG, c, w)

    heard = rks[0]
    for j in range(1, BLOCKS):
        heard = jnp.minimum(heard, rks[j])
    flagged = jnp.min(jnp.min(heard, axis=0, keepdims=True), axis=1, keepdims=True) < 0.0

    def folded(block):
        lines = []
        for j in range(n // LANES):
            span = slice(j * LANES, (j + 1) * LANES)
            by_row = jnp.max(racc[block, span, :].T, axis=0, keepdims=True)
            lines.append(jnp.broadcast_to(jnp.maximum(by_row, jnp.max(cacc[block, :, span], axis=0, keepdims=True)), (8, LANES)))
        tile = jnp.where((lane == FLAG) & flagged, 2.0, -1.0)
        for i in range(NSLOT):
            for j in range(n // LANES):
                start = j * LANES - i * cap
                if -LANES < start < cap:
                    piece = lines[j]
                    if start % LANES:
                        piece = pltpu.roll(piece, start % LANES, 1)
                    tile = jnp.where((sub == i) & (lane >= start) & (lane < min(cap, start + LANES)), piece, tile)
        return tile

    ends = ((DIAG, at(y, k, zin, xp)), (lsel, at(y, xor(k, x // 2), z, xm)), (RIGHT + k, right),
            (rsel, at(y, xor(k, z % 2), z, xp)), (OWN + o, sibling))
    copies = []
    for j, (block, to) in enumerate(ends):
        part[j] = folded(block)
        copies.append(remote(part.at[j], rpart.at[j], sp.at[j], rp.at[j], to))
        copies[-1].start()
    best = folded(OWN + k)
    for j, copy in enumerate(copies):
        copy.wait_recv()
        best = jnp.maximum(best, rpart[j])
    fin[...] = best
    back = [None] + [remote(fin, home.at[i], sf.at[i], rf.at[i], source(i)) for i in range(1, NSLOT)]
    for i in reversed(range(1, NSLOT)):
        back[i].start()
    home[0] = best

    for i in range(1, NSLOT):
        rank1[i].wait_send()
    for u in units:
        if u in first:
            first[u].wait_send()
        for group in (to_left, to_right, to_sib, to_inner, sib_right, sib_left):
            group[u].wait_send()
    for copy in (rank_left, rank_right, rank_sib, rank_inner, rank_sib_right, rank_sib_left, *copies):
        copy.wait_send()

    lines = []
    for i in range(NSLOT):
        if i:
            back[i].wait_recv()
        value = home[i, i:i + 1, :]
        high = value.astype(jnp.bfloat16).astype(jnp.float32)
        middle = (value - high).astype(jnp.bfloat16).astype(jnp.float32)
        low = value - high - middle
        line = jnp.where(sub == 0, high, jnp.where(sub == 1, middle, jnp.where(sub == 2, low, 0.0)))
        lines.append(line.astype(jnp.bfloat16))
        if i % 2:
            found = jnp.dot(jnp.concatenate(lines, axis=1), pack[(i - 1) * LANES:(i + 1) * LANES, :], preferred_element_type=jnp.float32)
            picked = found if i == 1 else picked + found
            lines = []
    result = picked[0:1] + picked[1:2] + picked[2:3]
    over = jnp.max(best[0:1, FLAG:], axis=1, keepdims=True)
    out_ref[...] = result.reshape(DOC)
    flag_ref[...] = jnp.broadcast_to(over, (1, LANES)).reshape(LANES)
    for i in range(1, NSLOT):
        back[i].wait_send()


def nearest(cap, number, embeddings, routes, ranks):
    n = NSLOT * cap
    f32, bf16 = jnp.float32, jnp.bfloat16
    dma = pltpu.SemaphoreType.DMA
    vmem = pl.BlockSpec(memory_space=pltpu.VMEM)
    return pl.pallas_call(
        lambda *refs: kernel(cap, *refs),
        out_shape=[jax.ShapeDtypeStruct((DOC,), f32), jax.ShapeDtypeStruct((LANES,), f32)],
        in_specs=[pl.BlockSpec(memory_space=pl.ANY)] * 3,
        out_specs=[vmem, vmem],
        scratch_shapes=[
            pltpu.VMEM((1, DOC), jnp.int32),
            pltpu.VMEM((DOC,), jnp.int32),
            pltpu.VMEM((DOC, D), bf16),
            pltpu.VMEM((NSLOT * LANES, DOC), bf16),
            pltpu.VMEM((n, D), bf16),
            pltpu.VMEM((NSLOT, 8, LANES), f32),
            pltpu.VMEM((NSLOT, 8, LANES), f32),
            pltpu.VMEM((BLOCKS, n, D), bf16),
            pltpu.VMEM((BLOCKS, 8, LANES), f32),
            pltpu.VMEM((BLOCKS, 8, n), f32),
            pltpu.VMEM((BLOCKS, n, LANES), f32),
            pltpu.VMEM((BLOCKS, n, LANES), f32),
            pltpu.VMEM((BLOCKS, 8, n), f32),
            pltpu.VMEM((5, 8, LANES), f32),
            pltpu.VMEM((5, 8, LANES), f32),
            pltpu.VMEM((8, LANES), f32),
            pltpu.VMEM((NSLOT, 8, LANES), f32),
            dma((len(UNITS),)), dma((len(UNITS),)), dma((NSLOT,)), dma((NSLOT,)),
            dma((6, len(UNITS))), dma((6, len(UNITS))), dma((6,)), dma((6,)),
            dma((5,)), dma((5,)), dma((NSLOT,)), dma((NSLOT,)), dma((3,)),
        ],
        compiler_params=pltpu.CompilerParams(collective_id=number, has_side_effects=True, vmem_limit_bytes=56 * 2**20),
        cost_estimate=pl.CostEstimate(flops=17 * n * n * D, bytes_accessed=2 * DOC * D, transcendentals=DOC),
    )(embeddings, routes.reshape(1, DOC), ranks)


def body(embeddings, routes, ranks):
    quick, flag = nearest(64, 1, embeddings, routes, ranks)
    return lax.cond(flag[0] > 1.5, lambda: nearest(96, 2, embeddings, routes, ranks)[0], lambda: quick)


def solution(mesh):
    in_specs = (P(("grp", "blk"), None), P(("grp", "blk"), None), P(("grp", "blk")))
    return jax.shard_map(body, mesh=mesh, in_specs=in_specs, out_specs=P(("grp", "blk")), check_vma=False)
```

```python
import jax
import jax.numpy as jnp
from jax import lax
from jax.experimental import pallas as pl
from jax.experimental.pallas import tpu as pltpu
from jax.sharding import PartitionSpec as P

MESH = pl.DeviceIdType.MESH
D = 1024
DOC = 384
NSLOT = 8
LANES = 128
LATE = float(1 << 20)
DY = (0, 0, 1, 3, 1, 3, 2, 2)
ZZ = (0, 1, 0, 0, 1, 1, 0, 1)
OWN, LEFT, RIGHT, DIAG, BLOCKS = 0, 2, 4, 6, 7
GROUPS = ((0,), (1, 2, 3, 6), (7, 5, 4))
PIECES = 2
LAG = 5
RANKS = 10
UNITS = tuple((i, p) for group in GROUPS for p in range(PIECES) for i in group)
FLAG = LANES - 1


def xor(a, b):
    return a + b - 2 * a * b


def kernel(cap, emb_ref, route_ref, rank_ref, out_ref, flag_ref, routed, ranked, unit, pack, send, msg, seen, blk, rks, rcol, rrow, racc, cacc,
           part, rpart, fin, home, s1, r1, sk, rk, sx, rx, sq, rq, sp, rp, sf, rf, se):
    n = NSLOT * cap
    g, b = lax.axis_index("grp"), lax.axis_index("blk")
    y, k, z, x = g // 2, g % 2, b // 4, b % 4
    o = 1 - k
    zin, zout = z + 1 - 2 * (z % 2), 3 - z
    xp, xm = (x + 1) % 4, (x + 3) % 4
    lsel, rsel = LEFT + xor(k, x // 2), RIGHT + xor(k, z % 2)

    def at(yy, kk, zz, xx):
        return (yy * 2 + kk, zz * 4 + xx)

    def target(i):
        return at((y + DY[i]) % 4, k, zout if ZZ[i] else z, x)

    def source(i):
        return at((y + 4 - DY[i]) % 4, k, zout if ZZ[i] else z, x)

    left, right, sibling, inner = at(y, k, z, xm), at(y, k, z, xp), at(y, o, z, x), at(y, k, zin, x)

    def remote(src, dst, ss, rs, to):
        return pltpu.make_async_remote_copy(src_ref=src, dst_ref=dst, send_sem=ss, recv_sem=rs, device_id=to, device_id_type=MESH)

    loads = [pltpu.make_async_copy(src, dst, se.at[j]) for j, (src, dst) in enumerate(((route_ref, routed), (rank_ref, ranked), (emb_ref, unit)))]
    for load in loads:
        load.start()
    barrier = pltpu.get_barrier_semaphore()
    partners = [target(i) for i in range(1, NSLOT)] + [left, right, sibling, inner]
    partners += [at(y, o, z, xm), at(y, o, z, xp), at(y, k, zin, xm), at(y, k, zin, xp)]
    for to in partners:
        pl.semaphore_signal(barrier, inc=1, device_id=to, device_id_type=MESH)

    loads[0].wait()
    cluster = routed[...] // 16
    index = jnp.zeros((1, DOC), jnp.int32)
    for i in range(1, NSLOT):
        zz = zout if ZZ[i] else z
        index = jnp.where(cluster == ((y + DY[i]) % 4) * 2 + zz // 2, i, index)
    chosen = index == lax.broadcasted_iota(jnp.int32, (NSLOT, DOC), 0)
    onehot = jnp.where(chosen, 1.0, 0.0)
    before = lax.broadcasted_iota(jnp.int32, (DOC, DOC), 0) < lax.broadcasted_iota(jnp.int32, (DOC, DOC), 1)
    counts = jnp.dot(onehot.astype(jnp.bfloat16), jnp.where(before, 1.0, 0.0).astype(jnp.bfloat16),
                     preferred_element_type=jnp.float32)
    position = jnp.sum(counts * onehot, axis=0, keepdims=True).astype(jnp.int32)
    place = index * LANES + position
    most = jnp.max(position, axis=1, keepdims=True)
    for i in range(NSLOT):
        hit = place == lax.broadcasted_iota(jnp.int32, (LANES, DOC), 0) + i * LANES
        pack[i * LANES:(i + 1) * LANES, :] = jnp.where(hit, 1.0, 0.0).astype(jnp.bfloat16)

    loads[1].wait()
    rank = ranked[...].reshape(1, DOC)
    line = lax.broadcasted_iota(jnp.int32, (8, DOC), 0)
    digits = jnp.where(line == 0, rank // 256, jnp.where(line == 1, rank % 256, 1)).astype(jnp.float32).astype(jnp.bfloat16)
    placed = lax.dot_general(digits, pack[...], (((1,), (1,)), ((), ())), preferred_element_type=jnp.float32)
    slot_rank = placed[0:1] * 256.0 + placed[1:2] + (1.0 - placed[2:3]) * LATE
    sub, lane = lax.broadcasted_iota(jnp.int32, (8, LANES), 0), lax.broadcasted_iota(jnp.int32, (8, LANES), 1)
    for i in range(NSLOT):
        row = jnp.broadcast_to(slot_rank[:, i * LANES:(i + 1) * LANES], (8, LANES))
        row = jnp.where(lane < cap, row, jnp.where((lane == FLAG) & (most >= cap), -1.0, LATE))
        msg[i] = jnp.where(sub == i, row, LATE)
    seen[0] = msg[0]

    size = cap // PIECES

    loads[2].wait()
    values = unit[...].astype(jnp.float32)
    unit[...] = (values * lax.rsqrt(jnp.sum(values * values, axis=1, keepdims=True) + 1e-06)).astype(jnp.bfloat16)

    def rows(u):
        i, p = UNITS[u]
        return pl.ds(i * cap + p * size, size)

    units = range(len(UNITS))
    first = {u: remote(send.at[pl.ds(i * cap + p * size, size)], blk.at[OWN + k, rows(u)], s1.at[u], r1.at[u], target(i))
             for u, (i, p) in enumerate(UNITS) if i}
    rank1 = [None] + [remote(msg.at[i], seen.at[i], sk.at[i], rk.at[i], target(i)) for i in range(1, NSLOT)]

    def route(kind, src, dst, to):
        return [remote(blk.at[src, rows(u)], blk.at[dst, rows(u)], sx.at[kind, u], rx.at[kind, u], to) for u in units], \
            remote(rks.at[src], rks.at[dst], sq.at[kind], rq.at[kind], to)

    to_left, rank_left = route(0, OWN + k, RIGHT + k, left)
    to_right, rank_right = route(1, OWN + k, LEFT + k, right)
    to_sib, rank_sib = route(2, OWN + k, OWN + k, sibling)
    to_inner, rank_inner = route(3, RIGHT + k, DIAG, inner)
    sib_right, rank_sib_right = route(4, RIGHT + k, RIGHT + k, sibling)
    sib_left, rank_sib_left = route(5, LEFT + k, LEFT + k, sibling)

    pl.semaphore_wait(barrier, len(partners))

    places = jnp.concatenate([pack[i * LANES:i * LANES + cap, :] for i in range(NSLOT)], axis=0)
    blk[OWN + k, 0:cap, :] = jnp.dot(places[0:cap], unit[...], preferred_element_type=jnp.float32).astype(jnp.bfloat16)
    for u in range(PIECES):
        remote(blk.at[OWN + k, rows(u)], blk.at[DIAG, rows(u)], sx.at[3, u], rx.at[3, u], at(y, k, zin, xm)).start()
        to_right[u].start()
        to_sib[u].start()
    send[cap:, :] = jnp.dot(places[cap:], unit[...], preferred_element_type=jnp.float32).astype(jnp.bfloat16)
    for i in range(1, NSLOT):
        rank1[i].start()

    for u in units:
        if u in first:
            first[u].start()
    def spread(block):
        tile = rks[block]
        for j in range(n // LANES):
            line = jnp.full((8, LANES), LATE, jnp.float32)
            for i in range(NSLOT):
                start = i * cap - j * LANES
                if -cap < start < LANES:
                    piece = jnp.broadcast_to(tile[i:i + 1], (8, LANES))
                    if start % LANES:
                        piece = pltpu.roll(piece, start % LANES, 1)
                    line = jnp.where((lane >= start) & (lane < start + cap), piece, line)
            rcol[block, :, j * LANES:(j + 1) * LANES] = line
            rrow[block, j * LANES:(j + 1) * LANES, :] = jnp.broadcast_to(line[0:1], (LANES, LANES)).T

    def combine():
        for i in range(1, NSLOT):
            rank1[i].wait_recv()
        tile = seen[0]
        for i in range(1, NSLOT):
            tile = jnp.minimum(tile, seen[i])
        rks[OWN + k] = tile
        for copy in (rank_left, rank_right, rank_sib):
            copy.start()

    def relay(u):
        if u >= PIECES:
            to_left[u].wait_recv()
            to_inner[u].start()
            sib_right[u].start()
        to_right[u].wait_recv()
        sib_left[u].start()

    for u in range(PIECES, len(UNITS)):
        first[u].wait_recv()
        for copies in (to_left, to_right, to_sib):
            copies[u].start()
        if u == RANKS:
            combine()
        if u == RANKS + 3:
            rank_left.wait_recv()
            rank_inner.start()
            rank_sib_right.start()
            rank_right.wait_recv()
            rank_sib_left.start()
        if u >= LAG:
            relay(u - LAG)

    def many_rows(row_blocks, col_block, start, width):
        lines = [cacc[col_block, :, start + c:start + c + LANES] for c in range(0, width, LANES)]
        for row_block in row_blocks:
            score = lax.dot_general(blk[row_block], blk[col_block, start:start + width, :], (((1,), (1,)), ((), ())),
                                    preferred_element_type=jnp.float32)
            row_rank, best = rrow[row_block], racc[row_block]
            for j, c in enumerate(range(0, width, LANES)):
                part_score = score[:, c:c + LANES]
                keep = rcol[col_block, 0:1, start + c:start + c + LANES] < row_rank
                best = jnp.maximum(best, jnp.where(keep, part_score, -1.0))
                rest = jnp.where(keep, -1.0, part_score).reshape(n // 8, 8, LANES)
                lines[j] = jnp.maximum(lines[j], jnp.max(rest, axis=0))
            racc[row_block] = best
        for j, c in enumerate(range(0, width, LANES)):
            cacc[col_block, :, start + c:start + c + LANES] = lines[j]

    def block_pair(row_block, col_block, start, width, row_start=0, row_count=n, both=True):
        span = pl.ds(row_start, row_count)
        score = lax.dot_general(blk[row_block, span, :], blk[col_block, start:start + width, :], (((1,), (1,)), ((), ())),
                                preferred_element_type=jnp.float32)
        row_rank, best = rrow[row_block, span, :], racc[row_block, span, :]
        for c in range(0, width, LANES):
            col = slice(start + c, start + c + LANES)
            part_score = score[:, c:c + LANES]
            keep = rcol[col_block, 0:1, col] < row_rank
            best = jnp.maximum(best, jnp.where(keep, part_score, -1.0))
            if both:
                rest = jnp.where(keep, -1.0, part_score).reshape(row_count // 8, 8, LANES)
                cacc[col_block, :, col] = jnp.maximum(cacc[col_block, :, col], jnp.max(rest, axis=0))
        racc[row_block, span, :] = best

    chunks = [(c, min(256, n - c)) for c in range(0, n, 256)]

    def covered(c, w):
        return 1 + max(u for u, (i, p) in enumerate(UNITS) if i * cap + p * size < c + w)

    for u in range(PIECES):
        to_left[u].start()

    rsib = {kind: [remote(blk.at[dst, rows(u)], blk.at[dst, rows(u)], sx.at[kind, u], rx.at[kind, u], sibling) for u in units]
            for kind, dst in ((2, OWN + o), (4, RIGHT + o), (5, LEFT + o))}
    rsib_rank = {kind: remote(rks.at[dst], rks.at[dst], sq.at[kind], rq.at[kind], sibling)
                 for kind, dst in ((2, OWN + o), (4, RIGHT + o), (5, LEFT + o))}

    def own_rows(col_block, c, w):
        many_rows((OWN, OWN + 1), col_block, c, w)

    relays = list(range(len(UNITS) - LAG, len(UNITS)))

    def relay_next():
        if relays:
            relay(relays.pop(0))

    racc[...] = jnp.full(racc.shape, -1.0, jnp.float32)
    cacc[...] = jnp.full(cacc.shape, -1.0, jnp.float32)
    spread(OWN + k)
    for c, w in chunks:
        relay_next()
        block_pair(OWN + k, OWN + k, c, w, both=False)
    rsib_rank[2].wait_recv()
    spread(OWN + o)
    relay_next()
    for u in units:
        rsib[2][u].wait_recv()
    half = n // 2
    for c, w in chunks:
        block_pair(OWN, OWN + 1, c, w, row_start=pl.multiple_of(k * half, half), row_count=half)
    while relays:
        relay_next()
    rank_inner.wait_recv()
    spread(DIAG)
    early = covered(*chunks[0])
    for u in range(early):
        to_inner[u].wait_recv()
    own_rows(DIAG, *chunks[0])
    spread(RIGHT + k)
    for c, w in chunks[1:]:
        own_rows(RIGHT + k, c, w)
    spread(LEFT + k)
    rsib_rank[5].wait_recv()
    spread(LEFT + o)
    rsib_rank[4].wait_recv()
    spread(RIGHT + o)
    for u in range(PIECES):
        to_left[u].wait_recv()
        sib_right[u].start()
    own_rows(RIGHT + k, *chunks[0])
    for u in units:
        rsib[5][u].wait_recv()
    for c, w in chunks[1:]:
        block_pair(lsel, RIGHT + k, c, w)
    block_pair(lsel, RIGHT + k, *chunks[0])
    for u in units:
        rsib[4][u].wait_recv()

    def side_rows(c, w):
        many_rows((lsel, rsel), DIAG, c, w)

    side_rows(*chunks[0])
    for u in units[early:]:
        to_inner[u].wait_recv()
    for c, w in chunks[1:]:
        many_rows((OWN, OWN + 1, lsel, rsel), DIAG, c, w)

    heard = rks[0]
    for j in range(1, BLOCKS):
        heard = jnp.minimum(heard, rks[j])
    flagged = jnp.min(jnp.min(heard, axis=0, keepdims=True), axis=1, keepdims=True) < 0.0

    def folded(block):
        lines = []
        for j in range(n // LANES):
            span = slice(j * LANES, (j + 1) * LANES)
            by_row = jnp.max(racc[block, span, :].T, axis=0, keepdims=True)
            lines.append(jnp.broadcast_to(jnp.maximum(by_row, jnp.max(cacc[block, :, span], axis=0, keepdims=True)), (8, LANES)))
        tile = jnp.where((lane == FLAG) & flagged, 2.0, -1.0)
        for i in range(NSLOT):
            for j in range(n // LANES):
                start = j * LANES - i * cap
                if -LANES < start < cap:
                    piece = lines[j]
                    if start % LANES:
                        piece = pltpu.roll(piece, start % LANES, 1)
                    tile = jnp.where((sub == i) & (lane >= start) & (lane < min(cap, start + LANES)), piece, tile)
        return tile

    ends = ((DIAG, at(y, k, zin, xp)), (lsel, at(y, xor(k, x // 2), z, xm)), (RIGHT + k, right),
            (rsel, at(y, xor(k, z % 2), z, xp)), (OWN + o, sibling))
    copies = []
    for j, (block, to) in enumerate(ends):
        part[j] = folded(block)
        copies.append(remote(part.at[j], rpart.at[j], sp.at[j], rp.at[j], to))
        copies[-1].start()
    best = folded(OWN + k)
    for j, copy in enumerate(copies):
        copy.wait_recv()
        best = jnp.maximum(best, rpart[j])
    fin[...] = best
    back = [None] + [remote(fin, home.at[i], sf.at[i], rf.at[i], source(i)) for i in range(1, NSLOT)]
    for i in reversed(range(1, NSLOT)):
        back[i].start()
    home[0] = best

    for i in range(1, NSLOT):
        rank1[i].wait_send()
    for u in units:
        if u in first:
            first[u].wait_send()
        for group in (to_left, to_right, to_sib, to_inner, sib_right, sib_left):
            group[u].wait_send()
    for copy in (rank_left, rank_right, rank_sib, rank_inner, rank_sib_right, rank_sib_left, *copies):
        copy.wait_send()

    lines = []
    for i in range(NSLOT):
        if i:
            back[i].wait_recv()
        value = home[i, i:i + 1, :]
        high = value.astype(jnp.bfloat16).astype(jnp.float32)
        middle = (value - high).astype(jnp.bfloat16).astype(jnp.float32)
        low = value - high - middle
        line = jnp.where(sub == 0, high, jnp.where(sub == 1, middle, jnp.where(sub == 2, low, 0.0)))
        lines.append(line.astype(jnp.bfloat16))
        if i % 2:
            found = jnp.dot(jnp.concatenate(lines, axis=1), pack[(i - 1) * LANES:(i + 1) * LANES, :], preferred_element_type=jnp.float32)
            picked = found if i == 1 else picked + found
            lines = []
    result = picked[0:1] + picked[1:2] + picked[2:3]
    over = jnp.max(best[0:1, FLAG:], axis=1, keepdims=True)
    out_ref[...] = result.reshape(DOC)
    flag_ref[...] = jnp.broadcast_to(over, (1, LANES)).reshape(LANES)
    for i in range(1, NSLOT):
        back[i].wait_send()


def nearest(cap, number, embeddings, routes, ranks):
    n = NSLOT * cap
    f32, bf16 = jnp.float32, jnp.bfloat16
    dma = pltpu.SemaphoreType.DMA
    vmem = pl.BlockSpec(memory_space=pltpu.VMEM)
    return pl.pallas_call(
        lambda *refs: kernel(cap, *refs),
        out_shape=[jax.ShapeDtypeStruct((DOC,), f32), jax.ShapeDtypeStruct((LANES,), f32)],
        in_specs=[pl.BlockSpec(memory_space=pltpu.HBM)] * 3,
        out_specs=[vmem, vmem],
        scratch_shapes=[
            pltpu.VMEM((1, DOC), jnp.int32),
            pltpu.VMEM((DOC,), jnp.int32),
            pltpu.VMEM((DOC, D), bf16),
            pltpu.VMEM((NSLOT * LANES, DOC), bf16),
            pltpu.VMEM((n, D), bf16),
            pltpu.VMEM((NSLOT, 8, LANES), f32),
            pltpu.VMEM((NSLOT, 8, LANES), f32),
            pltpu.VMEM((BLOCKS, n, D), bf16),
            pltpu.VMEM((BLOCKS, 8, LANES), f32),
            pltpu.VMEM((BLOCKS, 8, n), f32),
            pltpu.VMEM((BLOCKS, n, LANES), f32),
            pltpu.VMEM((BLOCKS, n, LANES), f32),
            pltpu.VMEM((BLOCKS, 8, n), f32),
            pltpu.VMEM((5, 8, LANES), f32),
            pltpu.VMEM((5, 8, LANES), f32),
            pltpu.VMEM((8, LANES), f32),
            pltpu.VMEM((NSLOT, 8, LANES), f32),
            dma((len(UNITS),)), dma((len(UNITS),)), dma((NSLOT,)), dma((NSLOT,)),
            dma((6, len(UNITS))), dma((6, len(UNITS))), dma((6,)), dma((6,)),
            dma((5,)), dma((5,)), dma((NSLOT,)), dma((NSLOT,)), dma((3,)),
        ],
        compiler_params=pltpu.CompilerParams(collective_id=number, has_side_effects=True, vmem_limit_bytes=56 * 2**20),
        cost_estimate=pl.CostEstimate(flops=17 * n * n * D, bytes_accessed=2 * DOC * D, transcendentals=DOC),
    )(embeddings, routes.reshape(1, DOC), ranks)


def body(embeddings, routes, ranks):
    quick, flag = nearest(64, 1, embeddings, routes, ranks)
    return lax.cond(flag[0] > 1.5, lambda: nearest(96, 2, embeddings, routes, ranks)[0], lambda: quick)


def solution(mesh):
    in_specs = (P(("grp", "blk"), None), P(("grp", "blk"), None), P(("grp", "blk")))
    return jax.shard_map(body, mesh=mesh, in_specs=in_specs, out_specs=P(("grp", "blk")), check_vma=False)
```
